512 devices in a mesh: dp: 16 (over y, x), expert: 16 (over z), tensor: 2 (over core).
Axes of the slice: x: 4, y: 4, z: 16, core: 2. Of those that a mesh axis runs over, the one named last changes fastest.
Arguments:
- tokens: bfloat16 [4096, 3072], P(('expert', 'tensor')), may hold values from -6 to 6
- expert_ids: int32 [4096, 4], P('expert'), may hold values from 0 to 15, all different within a row; in each aligned block of 128 rows (0 to 127, 128 to 255, ...) at most 34 rows name the same one
- gate_values: float32 [4096, 4], P('expert'), may hold values from 0.1 to 1
- w_gate: bfloat16 [16, 5376, 3072], P('expert', ('dp', 'tensor')), may hold values from -0.109375 to 0.109375
- w_up: bfloat16 [16, 5376, 3072], P('expert', ('dp', 'tensor')), may hold values from -0.109375 to 0.109375
- w_down: bfloat16 [16, 5376, 3072], P('expert', ('dp', 'tensor')), may hold values from -0.15625 to 0.15625
Outputs:
- mixed: bfloat16 [4096, 3072], P(('expert', 'tensor'), 'dp')
The draws below stay inside these ranges and needn't reach their ends.
Inputs may be any that keep to these rules, and one draw needn't show every extreme that they name: `expert_ids`: each row names 4 different experts; in each aligned block of 128 rows (the rows of one device) no expert is named by more than 34 entries.
All inputs are finite; a program needn't handle non-finite values.
Results may differ from the reference program's by a relative error of at most 0.012.
Values may be sent and summed in bfloat16 or wider, within the bound.
No kernel may reach another device: no remote copies, remote signals or barrier semaphores. Data moves between devices by JAX's collectives and lax.ppermute only.
A program may use at most 128 MiB of HBM per device.

```python
import math
import jax
import jax.numpy as jnp
import numpy as np
from jax import lax

D = 3072
FF = 5376
EXPERTS = 16
TOP = 4
TOK_DEV = 128
CAP = 34
FF_DEV = 168
TOKENS = 4096


def spiked(entries, stream_key, source, target, shards_of, factor):
    def block_of(dim):
        return (jnp.arange(entries.shape[dim]) // (entries.shape[dim] // shards_of)).reshape((-1,) + (1,) * (entries.ndim - 1 - dim))

    near = jax.random.permutation(stream_key, shards_of)[block_of(target)]
    far = (block_of(target) + shards_of // 2) % shards_of
    return jnp.where((block_of(source) == near) | (block_of(source) == far), factor * entries, entries)


def block_levels(stream_key, shape, split, least, high):
    level, own = 1.0, jax.random.fold_in(stream_key, 6)
    for axis_at, shards_of in split:
        heights = jnp.exp(jax.random.uniform(jax.random.fold_in(own, axis_at), (shards_of,), jnp.float32, least / len(split), high / len(split)))
        level = level * jnp.repeat(heights, shape[axis_at] // shards_of).reshape([-1 if axis == axis_at else 1 for axis in range(len(shape))])
    return level


def deal_out(own_key, own, number, rows, number_of, top, most, skew):
    ranking = jax.random.permutation(own_key, number_of)
    crowded, common = load_shares(number_of, rows * top, most, skew, True), load_shares(number_of, rows * top, most, skew, False)
    places = jnp.arange(number_of)

    def named(sizes, rotation):
        used = int((sizes > 0).sum())
        fixed = max(1, used // 4)
        shifted = fixed + (places - fixed + rotation * (used - fixed)) % max(1, number_of - fixed)
        return jnp.zeros((number_of,), jnp.int32).at[ranking[jnp.where(places < fixed, places, shifted)]].set(jnp.asarray(sizes, jnp.int32))

    sizes = jnp.where(number % 4 == 0, named(crowded, number // 4), named(common, number - number // 4 - 1))
    mixed = jax.random.permutation(jax.random.fold_in(own, 3), number_of)
    donor, receiver = mixed[0:number_of // 2 * 2:2], mixed[1:number_of // 2 * 2:2]
    margin = jnp.minimum(sizes[donor] - 1, most - sizes[receiver]) // 2
    margin = jnp.where((donor == ranking[0]) | (receiver == ranking[0]) | (sizes[receiver] == 0), 0, jnp.maximum(margin, 0))
    shifted = jax.random.randint(jax.random.fold_in(own, 4), (number_of // 2,), 0, 1 << 20) % (margin + 1)
    sizes = sizes.at[donor].add(-shifted).at[receiver].add(shifted)
    items = jnp.searchsorted(jnp.cumsum(sizes), jnp.arange(rows * top), side="right").astype(jnp.int32)
    table = items.reshape(top, rows).T
    table = table[jax.random.permutation(jax.random.fold_in(own, 1), rows)]
    rotation = jax.random.randint(jax.random.fold_in(own, 2), (rows, 1), 0, top)
    return jnp.take_along_axis(table, (jnp.arange(top)[None, :] + rotation) % top, axis=1)


def load_shares(count, total, limit, lean, full):
    loads = [(1 << 20) // math.isqrt(standing ** lean) + 1 for standing in range(1, count + 1)]
    largest = limit if full else min(limit, max(-(-total // count), total * loads[0] // sum(loads)))
    least = 1 if total - largest >= count - 1 else 0
    holding, rest = [largest] + [least] * (count - 1), total - largest - least * (count - 1)
    while rest > 0:
        free = [i for i in range(1, count) if holding[i] < largest] or [i for i in range(1, count) if holding[i] < limit]
        mass, left = sum([loads[i] for i in free]), rest
        for i in free:
            addition = min(limit - holding[i], max(1, left * loads[i] // mass), rest)
            holding[i] = holding[i] + addition
            rest = rest - addition
    return np.array(holding)


def noise(key, shape, width, reach, cuts=(), kind=jnp.bfloat16):
    drawn = width * jax.random.normal(key, shape, jnp.float32)
    if cuts:
        drawn = drawn * block_levels(key, shape, cuts, -0.22, 0.18)
    return jnp.clip(drawn, -reach, reach).astype(kind)


def gaussian_with(stream_key, shape, width, most, shards, heavy, kind=jnp.bfloat16):
    entries = width * jax.random.normal(stream_key, shape, jnp.float32)
    if shards:
        entries = entries * block_levels(stream_key, shape, shards, -0.22, 0.18)
    return jnp.clip(spiked(entries, jax.random.fold_in(stream_key, 3), *heavy), -most, most).astype(kind)


def setup_inputs(seed: int = 0) -> dict:
    seeds = jax.random.split(jax.random.key(seed), 7)
    tokens = noise(seeds[0], (TOKENS, D), 1.0, 6.0, ((0, 32),))
    expert_ids_keys = jax.random.split(jax.random.fold_in(seeds[1], 1), TOKENS // TOK_DEV)
    expert_ids_turns = jax.random.permutation(jax.random.fold_in(seeds[1], 3), TOKENS // TOK_DEV)
    expert_ids = jax.vmap(lambda own, number: deal_out(jax.random.fold_in(seeds[1], 2), own, number, TOK_DEV, EXPERTS, TOP, CAP, 2))(expert_ids_keys, expert_ids_turns).reshape((TOKENS, TOP))
    gate_values = jnp.clip(0.1 + 0.9 * jax.random.uniform(seeds[2], (TOKENS, TOP), jnp.float32) ** block_levels(seeds[2], (TOKENS, TOP), ((0, 16),), -0.2, 0.2), 0.1, 1.0)
    w_gate = noise(seeds[3], (EXPERTS, FF, D), D ** -0.5, 0.109375, ((0, 16), (1, 32)))
    w_up = noise(seeds[4], (EXPERTS, FF, D), D ** -0.5, 0.109375, ((0, 16), (1, 32)))
    w_down = gaussian_with(seeds[5], (EXPERTS, FF, D), FF ** -0.5, 0.15625, ((0, 16), (1, 32)), (1, 2, 32, 2.75))
    return dict(tokens=tokens, expert_ids=expert_ids, gate_values=gate_values, w_gate=w_gate, w_up=w_up, w_down=w_down)


def project_rows(rows, weight):
    return lax.dot_general(rows, weight, (((1,), (1,)), ((), ())), preferred_element_type=jnp.float32)


def reference(tokens, expert_ids, gate_values, w_gate, w_up, w_down):
    blocks = TOKENS // TOK_DEV
    id_blocks = expert_ids.reshape(blocks, TOK_DEV * TOP)
    onehot = (id_blocks[:, :, None] == jnp.arange(EXPERTS, dtype=jnp.int32)[None, None, :]).astype(jnp.int32)
    ranked = jnp.cumsum(onehot, axis=1) - onehot
    slot_ids = jnp.sum(ranked * onehot, axis=2).astype(jnp.int32)
    owners = jnp.repeat(jnp.arange(TOKENS, dtype=jnp.int32), TOP).reshape(blocks, TOK_DEV * TOP)
    block_index = jnp.broadcast_to(jnp.arange(blocks, dtype=jnp.int32)[:, None], (blocks, TOK_DEV * TOP))
    tables = jnp.full((EXPERTS, blocks, CAP), TOKENS, jnp.int32).at[id_blocks, block_index, slot_ids].set(owners)
    padded = jnp.concatenate([tokens, jnp.zeros((1, D), tokens.dtype)], axis=0)
    group_count = FF // FF_DEV

    def one_expert(operands):
        row_index, gate_w, up_w, down_w = operands
        expert_rows = padded[row_index.reshape(-1)]
        gate_act = project_rows(expert_rows, gate_w)
        up_act = project_rows(expert_rows, up_w)
        hidden = (jax.nn.silu(gate_act) * up_act).astype(jnp.bfloat16)

        def add_group(group_id, running):
            start = (group_id * FF_DEV).astype(jnp.int32)
            hidden_part = lax.dynamic_slice_in_dim(hidden, start, FF_DEV, 1)
            down_part = lax.dynamic_slice_in_dim(down_w, start, FF_DEV, 0)
            partial_out = jnp.dot(hidden_part, down_part, preferred_element_type=jnp.float32).astype(jnp.bfloat16)
            partial_out = lax.optimization_barrier(partial_out)
            return running + partial_out.astype(jnp.float32)

        return lax.fori_loop(0, group_count, add_group, jnp.zeros((blocks * CAP, D), jnp.float32))

    outputs = lax.map(one_expert, (tables, w_gate, w_up, w_down))
    flat_out = outputs.reshape(EXPERTS * blocks * CAP, D)
    token_block = (jnp.arange(TOKENS, dtype=jnp.int32) // TOK_DEV)[:, None]
    positions = expert_ids * (blocks * CAP) + token_block * CAP + slot_ids.reshape(TOKENS, TOP)
    picked = flat_out[positions.reshape(-1)].reshape(TOKENS, TOP, D)
    mixed = jnp.sum(gate_values[:, :, None] * picked, axis=1)
    return mixed.astype(jnp.bfloat16)
```

```python
import jax
import jax.numpy as jnp
from jax import lax
from jax.experimental import pallas as pl
from jax.experimental.pallas import tpu as pltpu
from jax.sharding import PartitionSpec as P

EXPERTS = 16
TOP = 4
CAP = 34
HALF = CAP // 2
DP = 16
VMEM = 60 * 1024 * 1024
F32 = jnp.float32
BF16 = jnp.bfloat16


def dot(a, b):
    return jnp.dot(a, b, preferred_element_type=F32)


def dot_t(a, b):
    return lax.dot_general(a, b, (((1,), (1,)), ((), ())), preferred_element_type=F32)


def row_places(shape, dim):
    row = lax.broadcasted_iota(jnp.int32, shape, dim).astype(F32)
    expert = jnp.floor((row + 0.5) * (1.0 / HALF))
    return expert, row - HALF * expert


def dispatch_kernel(ids_ref, rows_ref, out_ref):
    n = ids_ref.shape[1]
    experts = lax.broadcasted_iota(jnp.int32, (EXPERTS, n), 0)
    named = jnp.zeros((EXPERTS, n), F32)
    for k in range(TOP):
        named += (ids_ref[k : k + 1, :] == experts).astype(F32)
    earlier = lax.broadcasted_iota(jnp.int32, (n, n), 0) < lax.broadcasted_iota(jnp.int32, (n, n), 1)
    rank = dot(named.astype(BF16), earlier.astype(BF16))
    key = jnp.where(named > 0.0, rank, -1.0)
    expert, _ = row_places((EXPERTS * HALF, EXPERTS), 0)
    spread = (expert == lax.broadcasted_iota(jnp.int32, (EXPERTS * HALF, EXPERTS), 1).astype(F32)).astype(BF16)
    wide = dot(spread, key.astype(BF16))
    _, s = row_places((EXPERTS * HALF, n), 0)
    first = dot((wide == s).astype(BF16), rows_ref[...])
    second = dot((wide == s + HALF).astype(BF16), rows_ref[...])
    out_ref[...] = jnp.concatenate([first, second], axis=1).astype(BF16)


def expert_kernel(x_ref, gate0, up0, down0, gate1, up1, down1, out_ref, rows):
    parts, half_rows, two = x_ref.shape
    width = two // 2
    for side in range(2):
        for d in range(parts):
            rows[side * half_rows : (side + 1) * half_rows, d * width : (d + 1) * width] = x_ref[
                d, :, side * width : (side + 1) * width
            ]
    for side in range(2):
        x = rows[side * half_rows : (side + 1) * half_rows, :]
        total = None
        for gate, up, down in ((gate0, up0, down0), (gate1, up1, down1)):
            g = dot_t(x, gate[...])
            u = dot_t(x, up[...])
            hidden = (g / (1.0 + jnp.exp(-g)) * u).astype(BF16)
            part = dot(hidden, down[...])
            total = part if total is None else total + part
        y = total.astype(BF16)
        for d in range(parts):
            out_ref[d, :, side * width : (side + 1) * width] = y[:, d * width : (d + 1) * width]


def combine_kernel(ids_ref, gates_ref, rows_ref, out_ref):
    n = ids_ref.shape[0]
    width = out_ref.shape[1]
    experts = lax.broadcasted_iota(jnp.int32, (n, EXPERTS), 1)
    named = jnp.zeros((n, EXPERTS), F32)
    gates = jnp.zeros((n, EXPERTS), F32)
    for k in range(TOP):
        hit = (ids_ref[:, k : k + 1] == experts).astype(F32)
        named += hit
        gates += hit * gates_ref[:, k : k + 1]
    earlier = lax.broadcasted_iota(jnp.int32, (n, n), 1) < lax.broadcasted_iota(jnp.int32, (n, n), 0)
    rank = dot(earlier.astype(BF16), named.astype(BF16))
    key = jnp.where(named > 0.0, rank, -1.0)
    expert, _ = row_places((EXPERTS, EXPERTS * HALF), 1)
    spread = (expert == lax.broadcasted_iota(jnp.int32, (EXPERTS, EXPERTS * HALF), 0).astype(F32)).astype(BF16)
    wide = dot(key.astype(BF16), spread)
    _, s = row_places((n, EXPERTS * HALF), 1)
    first, second = wide == s, wide == s + HALF
    total = jnp.zeros((n, width), F32)
    for _ in range(3):
        piece = gates.astype(BF16)
        gates = gates - piece.astype(F32)
        weight = dot(piece, spread)
        total += dot(jnp.where(first, weight, 0.0).astype(BF16), rows_ref[:, :width])
        total += dot(jnp.where(second, weight, 0.0).astype(BF16), rows_ref[:, width:])
    out_ref[...] = total.astype(BF16)


def call(kernel, out, *args, scratch=()):
    return pl.pallas_call(
        kernel,
        out_shape=out,
        scratch_shapes=scratch,
        compiler_params=pltpu.CompilerParams(vmem_limit_bytes=VMEM),
    )(*args)


def swap(value):
    return lax.ppermute(value, "tensor", [(0, 1), (1, 0)])


def exchange(value, axis):
    return lax.all_to_all(value, axis, split_axis=0, concat_axis=0, tiled=True)


def shards(tokens, expert_ids, gate_values, w_gate, w_up, w_down):
    n, width = tokens.shape
    part = width // DP
    slots = EXPERTS * HALF
    core, place = lax.axis_index("tensor"), lax.axis_index("dp")
    weights = [w_gate[0], w_up[0], w_down[0]]
    others = [swap(w) for w in weights]
    ids = lax.dynamic_slice_in_dim(expert_ids, core * n, n, 0)
    gates = lax.dynamic_slice_in_dim(gate_values, core * n, n, 0)
    own = lax.dynamic_slice_in_dim(tokens, place * part, part, 1)
    sent = call(dispatch_kernel, jax.ShapeDtypeStruct((slots, 2 * part), BF16), ids.T, own)
    arrived = exchange(sent.reshape(EXPERTS, HALF, 2 * part), "expert").reshape(1, slots, 2 * part)
    rows = exchange(jnp.broadcast_to(arrived, (DP, slots, 2 * part)), "dp")
    partial = call(
        expert_kernel,
        jax.ShapeDtypeStruct((DP, slots, 2 * part), BF16),
        rows,
        *weights,
        *others,
        scratch=[pltpu.VMEM((2 * slots, width), BF16)],
    )
    partial = exchange(partial, "dp")
    summed = jnp.sum(partial.astype(F32), axis=0).astype(BF16)
    back = exchange(summed.reshape(EXPERTS, HALF, 2 * part), "expert").reshape(slots, 2 * part)
    return call(combine_kernel, jax.ShapeDtypeStruct((n, part), BF16), ids, gates, back)


def solution(mesh):
    placed = (
        P(("expert", "tensor"), None),
        P("expert", None),
        P("expert", None),
        P("expert", ("dp", "tensor"), None),
        P("expert", ("dp", "tensor"), None),
        P("expert", ("dp", "tensor"), None),
    )
    return jax.shard_map(
        shards, mesh=mesh, in_specs=placed, out_specs=P(("expert", "tensor"), "dp"), check_vma=False
    )
```

```python
import jax
import jax.numpy as jnp
from jax import lax
from jax.experimental import pallas as pl
from jax.experimental.pallas import tpu as pltpu
from jax.sharding import PartitionSpec as P

EXPERTS = 16
TOP = 4
CAP = 34
HALF = CAP // 2
SIZE = 4
DP = SIZE * SIZE
LANES = 128
HLANES = 64
BLOCK = 56
SIDE = EXPERTS * HALF
PART = 3 * SIDE
F32 = jnp.float32
BF16 = jnp.bfloat16


def quarter(y, x, core):
    a, b = (y + core) % SIZE, (x + core) % SIZE
    return a // 2 * 2 + b // 2, a % 2 * 2 + b % 2


def device(y, x, core):
    return (y % SIZE * SIZE + x % SIZE) * 2 + core


def quarter_groups():
    groups = {}
    for core in range(2):
        for y in range(SIZE):
            for x in range(SIZE):
                q, at = quarter(y, x, core)
                groups.setdefault((core, q), [0] * 4)[at] = device(y, x, core)
    return [groups[key] for key in sorted(groups)]


def across(mask):
    pairs = []
    for core in range(2):
        for y in range(SIZE):
            for x in range(SIZE):
                up = y + 1 if (y + core) % 2 else y - 1
                right = x + 1 if (x + core) % 2 else x - 1
                pairs.append((device(y, x, core), device(up if mask & 2 else y, right if mask & 1 else x, core)))
    return pairs


def dot(a, b):
    return jnp.dot(a, b, preferred_element_type=F32)


def dot_t(a, b):
    return lax.dot_general(a, b, (((1,), (1,)), ((), ())), preferred_element_type=F32)


def t_dot(a, b):
    return lax.dot_general(a, b, (((0,), (0,)), ((), ())), preferred_element_type=F32)


def iota(shape, dim):
    return lax.broadcasted_iota(jnp.int32, shape, dim)


def slot_picks(ids):
    n = ids.shape[1]
    named = jnp.zeros((EXPERTS, n), F32)
    for k in range(TOP):
        named += (ids[k : k + 1, :] == iota((EXPERTS, n), 0)).astype(F32)
    earlier = (iota((n, n), 0) < iota((n, n), 1)).astype(BF16)
    slot = jnp.where(named > 0.0, dot(named.astype(BF16), earlier), -1.0)
    rows = EXPERTS * BLOCK

    def expert_of(shape):
        return jnp.floor((iota(shape, 0).astype(F32) + 0.5) * (1.0 / BLOCK))

    spread = (expert_of((rows, EXPERTS)) == iota((rows, EXPERTS), 1).astype(F32)).astype(BF16)
    wide = dot(spread, slot.astype(BF16))
    at = iota((rows, n), 0).astype(F32) - BLOCK * expert_of((rows, n))
    main, half = at < CAP, (at >= CAP) & (at < CAP + HALF)
    return [main & (wide == at), half & (wide == at - CAP), half & (wide == at - HALF)], spread


def dispatch_kernel(ids_ref, tokens_ref, out_ref):
    n = tokens_ref.shape[0]
    core, dp = lax.axis_index("tensor"), lax.axis_index("dp")
    q, at = quarter(dp // SIZE, dp % SIZE, core)
    part = 4 * q + at
    picks, _ = slot_picks(ids_ref[:, pl.ds(pl.multiple_of(core * n, n), n)])
    picks = jnp.concatenate([p.astype(BF16) for p in picks], axis=1)
    first = tokens_ref[:, pl.ds(pl.multiple_of(part * LANES, LANES), LANES)]
    rest = tokens_ref[:, pl.ds(pl.multiple_of((DP + part // 2) * LANES, LANES), LANES)].astype(F32)
    low = iota((n, LANES), 1) < HLANES
    turned = pltpu.roll(rest, HLANES, 1)
    odd = part % 2 == 1
    here = jnp.where(odd, turned, rest)
    there = jnp.where(odd, rest, turned)
    rows = jnp.concatenate(
        [first, jnp.where(low, here, 0.0).astype(BF16), jnp.where(low, 0.0, there).astype(BF16)], axis=0
    )
    out_ref[...] = dot(picks, rows).astype(BF16)


def pack_kernel(blocks_ref, out_ref, source, packed):
    source[...] = blocks_ref[...].astype(F32)
    for e in range(EXPERTS):
        for third in range(3):
            packed[third * SIDE + e * HALF : third * SIDE + (e + 1) * HALF, :] = source[
                e * BLOCK + third * HALF : e * BLOCK + (third + 1) * HALF, :
            ]
    value = packed[...].astype(BF16)
    for copy in range(out_ref.shape[0]):
        out_ref[copy] = value


def expert_kernel(x0, x1, x2, x3, weights_ref, down_ref, out0, out1, out2, out3, rows):
    core, own = lax.axis_index("tensor"), lax.axis_index("dp")
    q, _ = quarter(own // SIZE, own % SIZE, core)
    hidden_width = down_ref.shape[0]
    low = iota((SIDE, LANES), 1) < HLANES
    for mask, x_ref in enumerate((x0, x1, x2, x3)):
        part = 4 * (q ^ mask)
        for at in range(4):
            rows[:, pl.ds(pl.multiple_of((part + at) * LANES, LANES), LANES)] = x_ref[at, : 2 * SIDE, :]
        for pair in range(2):
            even = x_ref[2 * pair, 2 * SIDE :, :].astype(F32)
            odd = x_ref[2 * pair + 1, 2 * SIDE :, :].astype(F32)
            lanes = pl.ds(pl.multiple_of((DP + part // 2 + pair) * LANES, LANES), LANES)
            rows[:SIDE, lanes] = jnp.where(low, even, pltpu.roll(odd, HLANES, 1)).astype(BF16)
            rows[SIDE:, lanes] = jnp.where(low, pltpu.roll(even, HLANES, 1), odd).astype(BF16)
    x = rows[...]
    g = dot_t(x, weights_ref[:hidden_width, :])
    u = dot_t(x, weights_ref[hidden_width:, :])
    hidden = (g / (1.0 + jnp.exp(-g)) * u).astype(BF16)
    for mask, out_ref in ((3, out3), (1, out1), (2, out2), (0, out0)):
        to = q ^ mask
        for at in range(4):
            dp = (to // 2 * 2 + at // 2 - core) % SIZE * SIZE + (to % 2 * 2 + at % 2 - core) % SIZE
            odd = dp % 2 == 1
            y = dot(hidden, down_ref[:, pl.ds(pl.multiple_of((dp * 3 - dp % 2) // 2 * LANES, LANES), 2 * LANES)])
            first, second = y[:, :LANES], y[:, LANES:]
            out_ref[at, : 2 * SIDE, :] = jnp.where(odd, second, first).astype(BF16)
            half = jnp.where(odd, first, second)
            turned = pltpu.roll(half, HLANES, 1)
            left, right = jnp.where(odd, turned, half), jnp.where(odd, half, turned)
            out_ref[at, 2 * SIDE :, :] = jnp.where(low, left[:SIDE], right[SIDE:]).astype(BF16)


def add_kernel(a, b, c, d, out_ref):
    out_ref[...] = (a[...].astype(F32) + b[...].astype(F32) + c[...].astype(F32) + d[...].astype(F32)).astype(BF16)


def add_blocks_kernel(parts_ref, out_ref, packed, blocks):
    total = parts_ref[0].astype(F32)
    for i in range(1, parts_ref.shape[0]):
        total += parts_ref[i].astype(F32)
    packed[...] = total
    for e in range(EXPERTS):
        for third in range(3):
            blocks[e * BLOCK + third * HALF : e * BLOCK + (third + 1) * HALF, :] = packed[
                third * SIDE + e * HALF : third * SIDE + (e + 1) * HALF, :
            ]
        blocks[e * BLOCK + 3 * HALF : (e + 1) * BLOCK, :] = jnp.zeros((BLOCK - 3 * HALF, LANES), F32)
    out_ref[...] = blocks[...].astype(BF16)


def combine_kernel(ids_ref, gates_ref, blocks_ref, out_ref):
    n = out_ref.shape[1]
    core, dp = lax.axis_index("tensor"), lax.axis_index("dp")
    own = pl.ds(pl.multiple_of(core * n, n), n)
    ids, given = ids_ref[:, own], gates_ref[:, own]
    picks, spread = slot_picks(ids)
    picks = jnp.concatenate(picks, axis=1)
    gates = jnp.zeros((EXPERTS, n), F32)
    for k in range(TOP):
        gates += jnp.where(ids[k : k + 1, :] == iota((EXPERTS, n), 0), given[k : k + 1, :], 0.0)
    total = jnp.zeros((LANES, 3 * n), F32)
    for _ in range(3):
        piece = gates.astype(BF16)
        gates = gates - piece.astype(F32)
        weight = dot(spread, piece)
        weight = jnp.concatenate([weight, weight, weight], axis=1)
        total += t_dot(blocks_ref[...], jnp.where(picks, weight, 0.0).astype(BF16))
    first = total[:, :n]
    rest = total[:HLANES, n : 2 * n] + total[HLANES:, 2 * n :]
    odd = dp % 2 == 1
    out_ref[:HLANES, :] = jnp.where(odd, rest, first[:HLANES]).astype(BF16)
    out_ref[HLANES:LANES, :] = jnp.where(odd, first[:HLANES], first[HLANES:]).astype(BF16)
    out_ref[LANES:, :] = jnp.where(odd, first[HLANES:], rest).astype(BF16)


def call(kernel, shape, *args, scratch=(), limit=16, outs=0):
    one = jax.ShapeDtypeStruct(shape, BF16)
    return pl.pallas_call(
        kernel,
        out_shape=[one] * outs if outs else one,
        scratch_shapes=scratch,
        compiler_params=pltpu.CompilerParams(vmem_limit_bytes=limit * 1024 * 1024),
    )(*args)


def swap(value):
    return lax.ppermute(value, "tensor", [(0, 1), (1, 0)])


def exchange(value, axis, groups=None):
    return lax.all_to_all(value, axis, split_axis=0, concat_axis=0, tiled=True, axis_index_groups=groups)


def shards(tokens, expert_ids, gate_values, w_gate, w_up, w_down):
    n, width = tokens.shape
    hidden = w_gate.shape[1]
    plane, inside = ("dp", "tensor"), quarter_groups()
    ids, gates = expert_ids.T, gate_values.T
    gap = jnp.zeros((-2 * hidden % LANES, width), BF16)
    gate, up, down = w_gate[0], w_up[0], w_down[0]
    weights = jnp.concatenate([gate, swap(gate), gap, up, swap(up), gap], axis=0)
    downs = jnp.concatenate([down, swap(down), gap], axis=0)
    part_scratch = pltpu.VMEM((PART, LANES), F32)
    block_scratch = pltpu.VMEM((EXPERTS * BLOCK, LANES), F32)

    sent = call(dispatch_kernel, (EXPERTS * BLOCK, LANES), ids, tokens)
    arrived = exchange(sent.reshape(EXPERTS, BLOCK, LANES), "expert").reshape(EXPERTS * BLOCK, LANES)
    rows = call(pack_kernel, (4, PART, LANES), arrived, scratch=[block_scratch, part_scratch])
    rows = exchange(rows, plane, inside)
    others = {mask: lax.ppermute(rows, plane, across(mask)) for mask in (3, 1, 2)}
    partial = call(
        expert_kernel,
        (4, PART, LANES),
        *(rows, others[1], others[2], others[3]),
        *(weights, downs),
        scratch=[pltpu.VMEM((2 * SIDE, width), BF16)],
        limit=48,
        outs=4,
    )
    others = {mask: lax.ppermute(partial[mask], plane, across(mask)) for mask in (3, 1, 2)}
    partial = call(add_kernel, (4, PART, LANES), partial[0], others[1], others[2], others[3], limit=24)
    partial = exchange(partial, plane, inside)
    summed = call(add_blocks_kernel, (EXPERTS * BLOCK, LANES), partial, scratch=[part_scratch, block_scratch])
    back = exchange(summed.reshape(EXPERTS, BLOCK, LANES), "expert").reshape(EXPERTS * BLOCK, LANES)
    return call(combine_kernel, (width // DP, n), ids, gates, back).T


def solution(mesh):
    placed = (
        P(("expert", "tensor"), None),
        P("expert", None),
        P("expert", None),
        P("expert", ("dp", "tensor"), None),
        P("expert", ("dp", "tensor"), None),
        P("expert", ("dp", "tensor"), None),
    )
    return jax.shard_map(
        shards, mesh=mesh, in_specs=placed, out_specs=P(("expert", "tensor"), "dp"), check_vma=False
    )
```

```python
import functools

import jax
import jax.numpy as jnp
from jax import lax
from jax.experimental import pallas as pl
from jax.experimental.pallas import tpu as pltpu
from jax.sharding import PartitionSpec as P

EXPERTS = 16
TOP = 4
CAP = 34
HALF = CAP // 2
SIZE = 4
DP = SIZE * SIZE
LANES = 128
HLANES = 64
BLOCK = 56
SIDE = EXPERTS * HALF
PART = 3 * SIDE
WIDE = 384
MASKS = (3, 1, 2)
F32 = jnp.float32
BF16 = jnp.bfloat16


def quarter(y, x, core):
    a, b = (y + core) % SIZE, (x + core) % SIZE
    return a // 2 * 2 + b // 2, a % 2 * 2 + b % 2


def device(y, x, core):
    return (y % SIZE * SIZE + x % SIZE) * 2 + core


def quarter_groups():
    groups = {}
    for core in range(2):
        for y in range(SIZE):
            for x in range(SIZE):
                q, at = quarter(y, x, core)
                groups.setdefault((core, q), [0] * 4)[at] = device(y, x, core)
    return [groups[key] for key in sorted(groups)]


def across(mask):
    pairs = []
    for core in range(2):
        for y in range(SIZE):
            for x in range(SIZE):
                up = y + 1 if (y + core) % 2 else y - 1
                right = x + 1 if (x + core) % 2 else x - 1
                pairs.append((device(y, x, core), device(up if mask & 2 else y, right if mask & 1 else x, core)))
    return pairs


def dot(a, b):
    return jnp.dot(a, b, preferred_element_type=F32)


def dot_t(a, b):
    return lax.dot_general(a, b, (((1,), (1,)), ((), ())), preferred_element_type=F32)


def t_dot(a, b):
    return lax.dot_general(a, b, (((0,), (0,)), ((), ())), preferred_element_type=F32)


def iota(shape, dim):
    return lax.broadcasted_iota(jnp.int32, shape, dim)


def slot_picks(ids):
    n = ids.shape[1]
    named = jnp.zeros((EXPERTS, n), F32)
    for k in range(TOP):
        named += (ids[k : k + 1, :] == iota((EXPERTS, n), 0)).astype(F32)
    earlier = (iota((n, n), 0) < iota((n, n), 1)).astype(BF16)
    slot = jnp.where(named > 0.0, dot(named.astype(BF16), earlier), -1.0)
    rows = EXPERTS * BLOCK

    def expert_of(shape):
        return jnp.floor((iota(shape, 0).astype(F32) + 0.5) * (1.0 / BLOCK))

    spread = (expert_of((rows, EXPERTS)) == iota((rows, EXPERTS), 1).astype(F32)).astype(BF16)
    wide = dot(spread, slot.astype(BF16))
    at = iota((rows, n), 0).astype(F32) - BLOCK * expert_of((rows, n))
    main, half = at < CAP, (at >= CAP) & (at < CAP + HALF)
    return [main & (wide == at), half & (wide == at - CAP), half & (wide == at - HALF)], spread


def dispatch_kernel(ids_ref, tokens_ref, out_ref):
    n = tokens_ref.shape[0]
    core, dp = lax.axis_index("tensor"), lax.axis_index("dp")
    q, at = quarter(dp // SIZE, dp % SIZE, core)
    part = 4 * q + at
    picks, _ = slot_picks(ids_ref[:, pl.ds(pl.multiple_of(core * n, n), n)])
    picks = jnp.concatenate([p.astype(BF16) for p in picks], axis=1)
    first = tokens_ref[:, pl.ds(pl.multiple_of(part * LANES, LANES), LANES)]
    rest = tokens_ref[:, pl.ds(pl.multiple_of((DP + part // 2) * LANES, LANES), LANES)].astype(F32)
    low = iota((n, LANES), 1) < HLANES
    turned = pltpu.roll(rest, HLANES, 1)
    odd = part % 2 == 1
    here = jnp.where(odd, turned, rest)
    there = jnp.where(odd, rest, turned)
    rows = jnp.concatenate(
        [first, jnp.where(low, here, 0.0).astype(BF16), jnp.where(low, 0.0, there).astype(BF16)], axis=0
    )
    out_ref[...] = dot(picks, rows).astype(BF16)


def pack_kernel(blocks_ref, out_ref, source, packed):
    source[...] = blocks_ref[...].astype(F32)
    for e in range(EXPERTS):
        for third in range(3):
            packed[third * SIDE + e * HALF : third * SIDE + (e + 1) * HALF, :] = source[
                e * BLOCK + third * HALF : e * BLOCK + (third + 1) * HALF, :
            ]
    value = packed[...].astype(BF16)
    for copy in range(out_ref.shape[0]):
        out_ref[copy] = value


def weights_kernel(gate0, up0, down0, gate1, up1, down1, weights_ref, down_ref):
    hidden, width = gate0.shape
    second = -(-hidden // 16) * 16
    for out_ref, at, pair in ((weights_ref, 0, (gate0, gate1)), (weights_ref, WIDE, (up0, up1)), (down_ref, 0, (down0, down1))):
        for start, ref, end in ((0, pair[0], second), (second, pair[1], WIDE)):
            out_ref[at + start : at + start + hidden, :] = ref[...]
            out_ref[at + start + hidden : at + end, :] = jnp.zeros((end - start - hidden, width), BF16)


def place_of():
    core, dp = lax.axis_index("tensor"), lax.axis_index("dp")
    return core, quarter(dp // SIZE, dp % SIZE, core)[0]


def products(mask, x_ref, weights_ref):
    _, q = place_of()
    q = q ^ mask
    low = iota((SIDE, LANES), 1) < HLANES
    main = jnp.concatenate([x_ref[at, : 2 * SIDE, :] for at in range(4)], axis=1)
    halves = []
    for pair in range(2):
        even = x_ref[2 * pair, 2 * SIDE :, :].astype(F32)
        odd = x_ref[2 * pair + 1, 2 * SIDE :, :].astype(F32)
        upper = jnp.where(low, even, pltpu.roll(odd, HLANES, 1)).astype(BF16)
        lower = jnp.where(low, pltpu.roll(even, HLANES, 1), odd).astype(BF16)
        halves.append(jnp.concatenate([upper, lower], axis=0))
    rest = jnp.concatenate(halves, axis=1)
    main_lanes = pl.ds(pl.multiple_of(q * 4 * LANES, LANES), 4 * LANES)
    rest_lanes = pl.ds(pl.multiple_of((DP + q * 2) * LANES, LANES), 2 * LANES)
    return dot_t(main, weights_ref[:, main_lanes]) + dot_t(rest, weights_ref[:, rest_lanes])


def down_products(mask, hidden, down_ref, out_ref):
    core, q = place_of()
    to = q ^ mask
    low = iota((SIDE, LANES), 1) < HLANES
    for at in range(4):
        dp = (to // 2 * 2 + at // 2 - core) % SIZE * SIZE + (to % 2 * 2 + at % 2 - core) % SIZE
        odd = dp % 2 == 1
        y = dot(hidden, down_ref[:, pl.ds(pl.multiple_of((dp * 3 - dp % 2) // 2 * LANES, LANES), 2 * LANES)])
        first, second = y[:, :LANES], y[:, LANES:]
        out_ref[at, : 2 * SIDE, :] = jnp.where(odd, second, first).astype(BF16)
        half = jnp.where(odd, first, second)
        turned = pltpu.roll(half, HLANES, 1)
        left, right = jnp.where(odd, turned, half), jnp.where(odd, half, turned)
        out_ref[at, 2 * SIDE :, :] = jnp.where(low, left[:SIDE], right[SIDE:]).astype(BF16)


def first_kernel(mask, x_ref, weights_ref, total_ref):
    total_ref[...] = products(mask, x_ref, weights_ref)


def next_kernel(mask, x_ref, weights_ref, sofar_ref, total_ref):
    total_ref[...] = sofar_ref[...] + products(mask, x_ref, weights_ref)


def last_kernel(mask, out_mask, x_ref, weights_ref, sofar_ref, down_ref, hidden_ref, out_ref):
    total = sofar_ref[...] + products(mask, x_ref, weights_ref)
    g, u = total[:, :WIDE], total[:, WIDE:]
    hidden = (g / (1.0 + jnp.exp(-g)) * u).astype(BF16)
    hidden_ref[...] = hidden
    down_products(out_mask, hidden, down_ref, out_ref)


def down_kernel(mask, hidden_ref, down_ref, out_ref):
    down_products(mask, hidden_ref[...], down_ref, out_ref)


def add_kernel(a, b, c, d, out_ref):
    out_ref[...] = (a[...].astype(F32) + b[...].astype(F32) + c[...].astype(F32) + d[...].astype(F32)).astype(BF16)


def add_blocks_kernel(parts_ref, out_ref, packed, blocks):
    total = parts_ref[0].astype(F32)
    for i in range(1, parts_ref.shape[0]):
        total += parts_ref[i].astype(F32)
    packed[...] = total
    for e in range(EXPERTS):
        for third in range(3):
            blocks[e * BLOCK + third * HALF : e * BLOCK + (third + 1) * HALF, :] = packed[
                third * SIDE + e * HALF : third * SIDE + (e + 1) * HALF, :
            ]
        blocks[e * BLOCK + 3 * HALF : (e + 1) * BLOCK, :] = jnp.zeros((BLOCK - 3 * HALF, LANES), F32)
    out_ref[...] = blocks[...].astype(BF16)


def combine_kernel(ids_ref, gates_ref, blocks_ref, out_ref):
    n = out_ref.shape[1]
    core, dp = lax.axis_index("tensor"), lax.axis_index("dp")
    own = pl.ds(pl.multiple_of(core * n, n), n)
    ids, given = ids_ref[:, own], gates_ref[:, own]
    picks, spread = slot_picks(ids)
    picks = jnp.concatenate(picks, axis=1)
    gates = jnp.zeros((EXPERTS, n), F32)
    for k in range(TOP):
        gates += jnp.where(ids[k : k + 1, :] == iota((EXPERTS, n), 0), given[k : k + 1, :], 0.0)
    total = jnp.zeros((LANES, 3 * n), F32)
    for _ in range(3):
        piece = gates.astype(BF16)
        gates = gates - piece.astype(F32)
        weight = dot(spread, piece)
        weight = jnp.concatenate([weight, weight, weight], axis=1)
        total += t_dot(blocks_ref[...], jnp.where(picks, weight, 0.0).astype(BF16))
    first = total[:, :n]
    rest = total[:HLANES, n : 2 * n] + total[HLANES:, 2 * n :]
    odd = dp % 2 == 1
    out_ref[:HLANES, :] = jnp.where(odd, rest, first[:HLANES]).astype(BF16)
    out_ref[HLANES:LANES, :] = jnp.where(odd, first[:HLANES], first[HLANES:]).astype(BF16)
    out_ref[LANES:, :] = jnp.where(odd, first[HLANES:], rest).astype(BF16)


def call(kernel, shape, *args, scratch=(), limit=16, dtype=BF16):
    out = jax.ShapeDtypeStruct(shape, dtype) if isinstance(shape, tuple) else [pltpu.VMEM(s, d) for s, d in shape]
    return pl.pallas_call(
        kernel,
        out_shape=out,
        scratch_shapes=scratch,
        compiler_params=pltpu.CompilerParams(vmem_limit_bytes=limit * 1024 * 1024),
    )(*args)


def held(value):
    return pltpu.with_memory_space_constraint(value, pltpu.VMEM)


def swap(value):
    return lax.ppermute(value, "tensor", [(0, 1), (1, 0)])


def exchange(value, axis, groups=None):
    return lax.all_to_all(value, axis, split_axis=0, concat_axis=0, tiled=True, axis_index_groups=groups)


def shards(tokens, expert_ids, gate_values, w_gate, w_up, w_down):
    n, width = tokens.shape
    plane, inside = ("dp", "tensor"), quarter_groups()
    ids, gates = expert_ids.T, gate_values.T
    own = [w_gate[0], w_up[0], w_down[0]]
    weights, down = call(
        weights_kernel, [((2 * WIDE, width), BF16), ((WIDE, width), BF16)], *own, *map(swap, own), limit=24
    )
    weights, down = held(weights), held(down)
    part_scratch = pltpu.VMEM((PART, LANES), F32)
    block_scratch = pltpu.VMEM((EXPERTS * BLOCK, LANES), F32)

    sent = call(dispatch_kernel, (EXPERTS * BLOCK, LANES), ids, tokens)
    arrived = exchange(sent.reshape(EXPERTS, BLOCK, LANES), "expert").reshape(EXPERTS * BLOCK, LANES)
    rows = call(pack_kernel, (4, PART, LANES), arrived, scratch=[block_scratch, part_scratch])
    rows = exchange(rows, plane, inside)
    others = [lax.ppermute(rows, plane, across(mask)) for mask in MASKS]
    total_shape, out_shape = ((2 * SIDE, 2 * WIDE), F32), ((4, PART, LANES), BF16)
    (total,) = call(functools.partial(first_kernel, 0), [total_shape], rows, weights, limit=32)
    for mask, other in zip(MASKS[:2], others[:2]):
        (total,) = call(functools.partial(next_kernel, mask), [total_shape], other, weights, held(total), limit=32)
    hidden, first = call(
        functools.partial(last_kernel, MASKS[2], MASKS[0]),
        [((2 * SIDE, WIDE), BF16), out_shape],
        *(others[2], weights, held(total), down),
        limit=32,
    )
    hidden = held(hidden)
    outs = [first]
    for mask in (*MASKS[1:], 0):
        outs += call(functools.partial(down_kernel, mask), [out_shape], hidden, down, limit=32)
    others = [lax.ppermute(out, plane, across(mask)) for mask, out in zip(MASKS, outs[:3])]
    partial = call(add_kernel, (4, PART, LANES), *others, outs[3], limit=24)
    partial = exchange(partial, plane, inside)
    summed = call(add_blocks_kernel, (EXPERTS * BLOCK, LANES), partial, scratch=[part_scratch, block_scratch])
    back = exchange(summed.reshape(EXPERTS, BLOCK, LANES), "expert").reshape(EXPERTS * BLOCK, LANES)
    return call(combine_kernel, (width // DP, n), ids, gates, back).T


def solution(mesh):
    placed = (
        P(("expert", "tensor"), None),
        P("expert", None),
        P("expert", None),
        P("expert", ("dp", "tensor"), None),
        P("expert", ("dp", "tensor"), None),
        P("expert", ("dp", "tensor"), None),
    )
    return jax.shard_map(
        shards, mesh=mesh, in_specs=placed, out_specs=P(("expert", "tensor"), "dp"), check_vma=False
    )
```

```python
import functools

import jax
import jax.numpy as jnp
from jax import lax
from jax.experimental import pallas as pl
from jax.experimental.pallas import tpu as pltpu
from jax.sharding import PartitionSpec as P

EXPERTS = 16
TOP = 4
CAP = 34
HALF = CAP // 2
SIZE = 4
DP = SIZE * SIZE
LANES = 128
HLANES = 64
RISE = 40
BLOCK = 56
SIDE = EXPERTS * HALF
PART = 3 * SIDE
AWAY = ((8, 4, -4, 0), (7, -7, 1, -1), (6, -6, 2, -2), (5, -5, 3, -3))
WIDE = 384
MASKS = (3, 1, 2)
F32 = jnp.float32
BF16 = jnp.bfloat16


def quarter(y, x, core):
    a, b = (y + core) % SIZE, (x + core) % SIZE
    return a // 2 * 2 + b // 2, a % 2 * 2 + b % 2


def device(y, x, core):
    return (y % SIZE * SIZE + x % SIZE) * 2 + core


def quarter_groups():
    groups = {}
    for core in range(2):
        for y in range(SIZE):
            for x in range(SIZE):
                q, at = quarter(y, x, core)
                groups.setdefault((core, q), [0] * 4)[at] = device(y, x, core)
    return [groups[key] for key in sorted(groups)]


def rising(k):
    pairs = []
    for y in range(SIZE):
        for x in range(SIZE):
            for z in range(EXPERTS):
                for core in range(2):
                    to = (z + AWAY[quarter(y, x, core)[1]][k]) % EXPERTS
                    at = (y * SIZE + x) * EXPERTS
                    pairs.append(((at + z) * 2 + core, (at + to) * 2 + core))
    return pairs


def across(mask):
    pairs = []
    for core in range(2):
        for y in range(SIZE):
            for x in range(SIZE):
                up = y + 1 if (y + core) % 2 else y - 1
                right = x + 1 if (x + core) % 2 else x - 1
                pairs.append((device(y, x, core), device(up if mask & 2 else y, right if mask & 1 else x, core)))
    return pairs


def dot(a, b):
    return jnp.dot(a, b, preferred_element_type=F32)


def dot_t(a, b):
    return lax.dot_general(a, b, (((1,), (1,)), ((), ())), preferred_element_type=F32)


def t_dot(a, b):
    return lax.dot_general(a, b, (((0,), (0,)), ((), ())), preferred_element_type=F32)


def iota(shape, dim):
    return lax.broadcasted_iota(jnp.int32, shape, dim)


def slots_of(ids):
    n = ids.shape[1]
    named = jnp.zeros((EXPERTS, n), F32)
    for k in range(TOP):
        named += (ids[k : k + 1, :] == iota((EXPERTS, n), 0)).astype(F32)
    earlier = (iota((n, n), 0) < iota((n, n), 1)).astype(BF16)
    return jnp.where(named > 0.0, dot(named.astype(BF16), earlier), -1.0).astype(BF16)


def place_of():
    core, dp = lax.axis_index("tensor"), lax.axis_index("dp")
    return core, *quarter(dp // SIZE, dp % SIZE, core)


def away_of(at, k):
    away = AWAY[0][k]
    for j in range(1, 4):
        away = jnp.where(at == j, AWAY[j][k], away)
    return away


def dispatch_kernel(ids_ref, tokens_ref, *out_refs):
    n, width = tokens_ref.shape
    core, q, at = place_of()
    slots = slots_of(ids_ref[:, pl.ds(pl.multiple_of(core * n, n), n)])
    part = width // 4
    rows = tokens_ref[:, pl.ds(pl.multiple_of(q * part, part), part)]
    for k, out_ref in enumerate(out_refs):
        expert = lax.rem(lax.axis_index("expert") + away_of(at, k) + EXPERTS, EXPERTS)
        spread = (iota((RISE, EXPERTS), 1) == expert).astype(BF16)
        picks = dot(spread, slots) == iota((RISE, n), 0).astype(F32)
        out_ref[...] = dot(picks.astype(BF16), rows).astype(BF16)


def pack_kernel(*refs):
    blocks, out_ref, packed = refs[:4], refs[4], refs[5]
    for k, ref in enumerate(blocks):
        packed[k * CAP : (k + 1) * CAP, :] = ref[...].astype(F32)[:CAP]
    value = packed[...].astype(BF16)
    for copy in range(out_ref.shape[0]):
        out_ref[copy] = value


def weights_kernel(gate0, up0, down0, gate1, up1, down1, weights_ref, down_ref):
    hidden, width = gate0.shape
    second = -(-hidden // 16) * 16
    for out_ref, at, pair in ((weights_ref, 0, (gate0, gate1)), (weights_ref, WIDE, (up0, up1)), (down_ref, 0, (down0, down1))):
        for start, ref, end in ((0, pair[0], second), (second, pair[1], WIDE)):
            out_ref[at + start : at + start + hidden, :] = ref[...]
            out_ref[at + start + hidden : at + end, :] = jnp.zeros((end - start - hidden, width), BF16)


def products(mask, x_ref, weights_ref):
    _, q, _ = place_of()
    part = x_ref.shape[1]
    lanes = pl.ds(pl.multiple_of((q ^ mask) * part, part), part)
    return dot_t(x_ref[...], weights_ref[:, lanes])


def down_products(mask, hidden, down_ref, out_ref):
    core, q, _ = place_of()
    to = q ^ mask
    low = iota((SIDE, LANES), 1) < HLANES
    for at in range(4):
        dp = (to // 2 * 2 + at // 2 - core) % SIZE * SIZE + (to % 2 * 2 + at % 2 - core) % SIZE
        odd = dp % 2 == 1
        y = dot(hidden, down_ref[:, pl.ds(pl.multiple_of((dp * 3 - dp % 2) // 2 * LANES, LANES), 2 * LANES)])
        first, second = y[:, :LANES], y[:, LANES:]
        out_ref[at, : 2 * SIDE, :] = jnp.where(odd, second, first).astype(BF16)
        half = jnp.where(odd, first, second)
        turned = pltpu.roll(half, HLANES, 1)
        left, right = jnp.where(odd, turned, half), jnp.where(odd, half, turned)
        out_ref[at, 2 * SIDE :, :] = jnp.where(low, left[:SIDE], right[SIDE:]).astype(BF16)


def first_kernel(mask, x_ref, weights_ref, total_ref):
    total_ref[...] = products(mask, x_ref, weights_ref)


def next_kernel(mask, x_ref, weights_ref, sofar_ref, total_ref):
    total_ref[...] = sofar_ref[...] + products(mask, x_ref, weights_ref)


def last_kernel(mask, out_mask, x_ref, weights_ref, sofar_ref, down_ref, hidden_ref, out_ref):
    total = sofar_ref[...] + products(mask, x_ref, weights_ref)
    g, u = total[:, :WIDE], total[:, WIDE:]
    hidden = (g / (1.0 + jnp.exp(-g)) * u).astype(BF16)
    hidden_ref[...] = hidden
    down_products(out_mask, hidden, down_ref, out_ref)


def down_kernel(mask, hidden_ref, down_ref, out_ref):
    down_products(mask, hidden_ref[...], down_ref, out_ref)


def add_kernel(a, b, c, d, out_ref):
    out_ref[...] = (a[...].astype(F32) + b[...].astype(F32) + c[...].astype(F32) + d[...].astype(F32)).astype(BF16)


def add_blocks_kernel(parts_ref, out_ref, packed, blocks):
    total = parts_ref[0].astype(F32)
    for i in range(1, parts_ref.shape[0]):
        total += parts_ref[i].astype(F32)
    packed[...] = total
    low = iota((HALF, LANES), 1) < HLANES

    def put(b, at, value):
        home = lax.rem(lax.axis_index("expert") - AWAY[b // 4][b % 4] + EXPERTS, EXPERTS)
        blocks[home, at : at + value.shape[0], :] = value

    for b in range(EXPERTS):
        put(b, 0, packed[b * CAP : (b + 1) * CAP, :])
        put(b, CAP + HALF, jnp.zeros((BLOCK - CAP - HALF, LANES), F32))
    for b in range(EXPERTS // 2):
        at = 2 * SIDE + b * CAP
        upper, lower = packed[at : at + HALF, :], packed[at + HALF : at + CAP, :]
        put(b, CAP, jnp.where(low, upper, pltpu.roll(lower, HLANES, 1)))
        put(b + EXPERTS // 2, CAP, jnp.where(low, pltpu.roll(upper, HLANES, 1), lower))
    for e in range(EXPERTS):
        out_ref[e] = blocks[e].astype(BF16)


def combine_kernel(ids_ref, gates_ref, blocks_ref, out_ref):
    n = out_ref.shape[1]
    core, dp = lax.axis_index("tensor"), lax.axis_index("dp")
    own = pl.ds(pl.multiple_of(core * n, n), n)
    ids, given = ids_ref[:, own], gates_ref[:, own]
    rows = EXPERTS * BLOCK

    def expert_of(shape):
        return jnp.floor((iota(shape, 0).astype(F32) + 0.5) * (1.0 / BLOCK))

    spread = (expert_of((rows, EXPERTS)) == iota((rows, EXPERTS), 1).astype(F32)).astype(BF16)
    wide = dot(spread, slots_of(ids))
    at = iota((rows, n), 0).astype(F32) - BLOCK * expert_of((rows, n))
    half = (at >= CAP) & (at < CAP + HALF)
    picks = jnp.concatenate(
        [(at < CAP) & (wide == at), half & (wide == at - CAP), half & (wide == at - HALF)], axis=1
    )
    gates = jnp.zeros((EXPERTS, n), F32)
    for k in range(TOP):
        gates += jnp.where(ids[k : k + 1, :] == iota((EXPERTS, n), 0), given[k : k + 1, :], 0.0)
    total = jnp.zeros((LANES, 3 * n), F32)
    for _ in range(3):
        piece = gates.astype(BF16)
        gates = gates - piece.astype(F32)
        weight = dot(spread, piece)
        weight = jnp.concatenate([weight, weight, weight], axis=1)
        total += t_dot(blocks_ref[...], jnp.where(picks, weight, 0.0).astype(BF16))
    first = total[:, :n]
    rest = total[:HLANES, n : 2 * n] + total[HLANES:, 2 * n :]
    odd = dp % 2 == 1
    out_ref[:HLANES, :] = jnp.where(odd, rest, first[:HLANES]).astype(BF16)
    out_ref[HLANES:LANES, :] = jnp.where(odd, first[:HLANES], first[HLANES:]).astype(BF16)
    out_ref[LANES:, :] = jnp.where(odd, first[HLANES:], rest).astype(BF16)


def call(kernel, shape, *args, scratch=(), limit=16, dtype=BF16):
    out = jax.ShapeDtypeStruct(shape, dtype) if isinstance(shape, tuple) else [pltpu.VMEM(s, d) for s, d in shape]
    return pl.pallas_call(
        kernel,
        out_shape=out,
        scratch_shapes=scratch,
        compiler_params=pltpu.CompilerParams(vmem_limit_bytes=limit * 1024 * 1024),
    )(*args)


def held(value):
    return pltpu.with_memory_space_constraint(value, pltpu.VMEM)


def swap(value):
    return lax.ppermute(value, "tensor", [(0, 1), (1, 0)])


def exchange(value, axis, groups=None):
    return lax.all_to_all(value, axis, split_axis=0, concat_axis=0, tiled=True, axis_index_groups=groups)


def shards(tokens, expert_ids, gate_values, w_gate, w_up, w_down):
    n, width = tokens.shape
    plane, inside = ("dp", "tensor"), quarter_groups()
    ids, gates = expert_ids.T, gate_values.T
    own = [w_gate[0], w_up[0], w_down[0]]
    weights, down = call(
        weights_kernel, [((2 * WIDE, width), BF16), ((WIDE, width), BF16)], *own, *map(swap, own), limit=24
    )
    weights, down = held(weights), held(down)
    part = width // 4
    sent = call(dispatch_kernel, [((RISE, part), BF16)] * 4, ids, tokens)
    arrived = [lax.ppermute(v, ("dp", "expert", "tensor"), rising(k)) for k, v in enumerate(sent)]
    rows = call(pack_kernel, (4, 4 * CAP, part), *arrived, scratch=[pltpu.VMEM((4 * CAP, part), F32)])
    rows = exchange(rows, plane, inside).reshape(2 * SIDE, part)
    others = [lax.ppermute(rows, plane, across(mask)) for mask in MASKS]
    total_shape, out_shape = ((2 * SIDE, 2 * WIDE), F32), ((4, PART, LANES), BF16)
    (total,) = call(functools.partial(first_kernel, 0), [total_shape], rows, weights, limit=32)
    for mask, other in zip(MASKS[:2], others[:2]):
        (total,) = call(functools.partial(next_kernel, mask), [total_shape], other, weights, held(total), limit=32)
    hidden, first = call(
        functools.partial(last_kernel, MASKS[2], MASKS[0]),
        [((2 * SIDE, WIDE), BF16), out_shape],
        *(others[2], weights, held(total), down),
        limit=32,
    )
    hidden = held(hidden)
    outs = [first]
    for mask in (*MASKS[1:], 0):
        outs += call(functools.partial(down_kernel, mask), [out_shape], hidden, down, limit=32)
    others = [lax.ppermute(out, plane, across(mask)) for mask, out in zip(MASKS, outs[:3])]
    partial = call(add_kernel, (4, PART, LANES), *others, outs[3], limit=24)
    partial = exchange(partial, plane, inside)
    summed = call(
        add_blocks_kernel,
        (EXPERTS, BLOCK, LANES),
        partial,
        scratch=[pltpu.VMEM((PART, LANES), F32), pltpu.VMEM((EXPERTS, BLOCK, LANES), F32)],
    )
    back = exchange(summed, "expert").reshape(EXPERTS * BLOCK, LANES)
    return call(combine_kernel, (width // DP, n), ids, gates, back).T


def solution(mesh):
    placed = (
        P(("expert", "tensor"), None),
        P("expert", None),
        P("expert", None),
        P("expert", ("dp", "tensor"), None),
        P("expert", ("dp", "tensor"), None),
        P("expert", ("dp", "tensor"), None),
    )
    return jax.shard_map(
        shards, mesh=mesh, in_specs=placed, out_specs=P(("expert", "tensor"), "dp"), check_vma=False
    )
```

```python
import functools

import jax
import jax.numpy as jnp
from jax import lax
from jax.experimental import pallas as pl
from jax.experimental.pallas import tpu as pltpu
from jax.sharding import PartitionSpec as P

EXPERTS = 16
TOP = 4
CAP = 34
HALF = CAP // 2
SIZE = 4
DP = SIZE * SIZE
LANES = 128
HLANES = 64
BLOCK = 56
SIDE = EXPERTS * HALF
PART = 3 * SIDE
WIDE = 384
MASKS = (3, 1, 2)
F32 = jnp.float32
BF16 = jnp.bfloat16


def quarter(y, x, core):
    a, b = (y + core) % SIZE, (x + core) % SIZE
    return a // 2 * 2 + b // 2, a % 2 * 2 + b % 2


def device(y, x, core):
    return (y % SIZE * SIZE + x % SIZE) * 2 + core


def quarter_groups():
    groups = {}
    for core in range(2):
        for y in range(SIZE):
            for x in range(SIZE):
                q, at = quarter(y, x, core)
                groups.setdefault((core, q), [0] * 4)[at] = device(y, x, core)
    return [groups[key] for key in sorted(groups)]


def across(mask):
    pairs = []
    for core in range(2):
        for y in range(SIZE):
            for x in range(SIZE):
                up = y + 1 if (y + core) % 2 else y - 1
                right = x + 1 if (x + core) % 2 else x - 1
                pairs.append((device(y, x, core), device(up if mask & 2 else y, right if mask & 1 else x, core)))
    return pairs


def dot(a, b):
    return jnp.dot(a, b, preferred_element_type=F32)


def dot_t(a, b):
    return lax.dot_general(a, b, (((1,), (1,)), ((), ())), preferred_element_type=F32)


def t_dot(a, b):
    return lax.dot_general(a, b, (((0,), (0,)), ((), ())), preferred_element_type=F32)


def iota(shape, dim):
    return lax.broadcasted_iota(jnp.int32, shape, dim)


def slot_picks(ids):
    n = ids.shape[1]
    named = jnp.zeros((EXPERTS, n), F32)
    for k in range(TOP):
        named += (ids[k : k + 1, :] == iota((EXPERTS, n), 0)).astype(F32)
    earlier = (iota((n, n), 0) < iota((n, n), 1)).astype(BF16)
    slot = jnp.where(named > 0.0, dot(named.astype(BF16), earlier), -1.0)
    rows = EXPERTS * BLOCK

    def expert_of(shape):
        return jnp.floor((iota(shape, 0).astype(F32) + 0.5) * (1.0 / BLOCK))

    spread = (expert_of((rows, EXPERTS)) == iota((rows, EXPERTS), 1).astype(F32)).astype(BF16)
    wide = dot(spread, slot.astype(BF16))
    at = iota((rows, n), 0).astype(F32) - BLOCK * expert_of((rows, n))
    main, half = at < CAP, (at >= CAP) & (at < CAP + HALF)
    return [main & (wide == at), half & (wide == at - CAP), half & (wide == at - HALF)], spread


def dispatch_kernel(ids_ref, tokens_ref, out_ref):
    n = tokens_ref.shape[0]
    core, dp = lax.axis_index("tensor"), lax.axis_index("dp")
    q, at = quarter(dp // SIZE, dp % SIZE, core)
    part = 4 * q + at
    picks, _ = slot_picks(ids_ref[:, pl.ds(pl.multiple_of(core * n, n), n)])
    picks = jnp.concatenate([p.astype(BF16) for p in picks], axis=1)
    first = tokens_ref[:, pl.ds(pl.multiple_of(part * LANES, LANES), LANES)]
    rest = tokens_ref[:, pl.ds(pl.multiple_of((DP + part // 2) * LANES, LANES), LANES)].astype(F32)
    low = iota((n, LANES), 1) < HLANES
    turned = pltpu.roll(rest, HLANES, 1)
    odd = part % 2 == 1
    here = jnp.where(odd, turned, rest)
    there = jnp.where(odd, rest, turned)
    rows = jnp.concatenate(
        [first, jnp.where(low, here, 0.0).astype(BF16), jnp.where(low, 0.0, there).astype(BF16)], axis=0
    )
    out_ref[...] = dot(picks, rows).astype(BF16)


def pack_kernel(blocks_ref, out_ref, source, packed):
    source[...] = blocks_ref[...].astype(F32)
    for e in range(EXPERTS):
        for third in range(3):
            packed[third * SIDE + e * HALF : third * SIDE + (e + 1) * HALF, :] = source[
                e * BLOCK + third * HALF : e * BLOCK + (third + 1) * HALF, :
            ]
    value = packed[...].astype(BF16)
    for copy in range(out_ref.shape[0]):
        out_ref[copy] = value


def weights_kernel(gate0, up0, down0, gate1, up1, down1, weights_ref, down_ref):
    hidden, width = gate0.shape
    second = -(-hidden // 16) * 16
    for out_ref, at, pair in ((weights_ref, 0, (gate0, gate1)), (weights_ref, WIDE, (up0, up1)), (down_ref, 0, (down0, down1))):
        for start, ref, end in ((0, pair[0], second), (second, pair[1], WIDE)):
            out_ref[at + start : at + start + hidden, :] = ref[...]
            out_ref[at + start + hidden : at + end, :] = jnp.zeros((end - start - hidden, width), BF16)


def place_of():
    core, dp = lax.axis_index("tensor"), lax.axis_index("dp")
    return core, quarter(dp // SIZE, dp % SIZE, core)[0]


def products(mask, x_ref, weights_ref):
    _, q = place_of()
    q = q ^ mask
    low = iota((SIDE, LANES), 1) < HLANES
    main = jnp.concatenate([x_ref[at, : 2 * SIDE, :] for at in range(4)], axis=1)
    halves = []
    for pair in range(2):
        even = x_ref[2 * pair, 2 * SIDE :, :].astype(F32)
        odd = x_ref[2 * pair + 1, 2 * SIDE :, :].astype(F32)
        upper = jnp.where(low, even, pltpu.roll(odd, HLANES, 1)).astype(BF16)
        lower = jnp.where(low, pltpu.roll(even, HLANES, 1), odd).astype(BF16)
        halves.append(jnp.concatenate([upper, lower], axis=0))
    rest = jnp.concatenate(halves, axis=1)
    main_lanes = pl.ds(pl.multiple_of(q * 4 * LANES, LANES), 4 * LANES)
    rest_lanes = pl.ds(pl.multiple_of((DP + q * 2) * LANES, LANES), 2 * LANES)
    return dot_t(main, weights_ref[:, main_lanes]) + dot_t(rest, weights_ref[:, rest_lanes])


def down_products(mask, hidden, down_ref, out_ref):
    core, q = place_of()
    to = q ^ mask
    low = iota((SIDE, LANES), 1) < HLANES
    for at in range(4):
        dp = (to // 2 * 2 + at // 2 - core) % SIZE * SIZE + (to % 2 * 2 + at % 2 - core) % SIZE
        odd = dp % 2 == 1
        y = dot(hidden, down_ref[:, pl.ds(pl.multiple_of((dp * 3 - dp % 2) // 2 * LANES, LANES), 2 * LANES)])
        first, second = y[:, :LANES], y[:, LANES:]
        out_ref[at, : 2 * SIDE, :] = jnp.where(odd, second, first).astype(BF16)
        half = jnp.where(odd, first, second)
        turned = pltpu.roll(half, HLANES, 1)
        left, right = jnp.where(odd, turned, half), jnp.where(odd, half, turned)
        out_ref[at, 2 * SIDE :, :] = jnp.where(low, left[:SIDE], right[SIDE:]).astype(BF16)


def first_kernel(mask, x_ref, weights_ref, total_ref):
    total_ref[...] = products(mask, x_ref, weights_ref)


def next_kernel(mask, x_ref, weights_ref, sofar_ref, total_ref):
    total_ref[...] = sofar_ref[...] + products(mask, x_ref, weights_ref)


def last_kernel(mask, out_mask, x_ref, weights_ref, sofar_ref, down_ref, hidden_ref, out_ref):
    total = sofar_ref[...] + products(mask, x_ref, weights_ref)
    g, u = total[:, :WIDE], total[:, WIDE:]
    hidden = (g / (1.0 + jnp.exp(-g)) * u).astype(BF16)
    hidden_ref[...] = hidden
    down_products(out_mask, hidden, down_ref, out_ref)


def down_kernel(mask, hidden_ref, down_ref, out_ref):
    down_products(mask, hidden_ref[...], down_ref, out_ref)


def add_kernel(a, b, out_ref):
    out_ref[...] = (a[...].astype(F32) + b[...].astype(F32)).astype(out_ref.dtype)


def add_blocks_kernel(parts_ref, out_ref, packed, blocks):
    total = parts_ref[0].astype(F32)
    for i in range(1, parts_ref.shape[0]):
        total += parts_ref[i].astype(F32)
    packed[...] = total
    for e in range(EXPERTS):
        for third in range(3):
            blocks[e * BLOCK + third * HALF : e * BLOCK + (third + 1) * HALF, :] = packed[
                third * SIDE + e * HALF : third * SIDE + (e + 1) * HALF, :
            ]
        blocks[e * BLOCK + 3 * HALF : (e + 1) * BLOCK, :] = jnp.zeros((BLOCK - 3 * HALF, LANES), F32)
    out_ref[...] = blocks[...].astype(BF16)


def gates_kernel(ids_ref, gates_ref, out_ref):
    n = out_ref.shape[2] // 3
    own = pl.ds(pl.multiple_of(lax.axis_index("tensor") * n, n), n)
    ids, given = ids_ref[:, own], gates_ref[:, own]
    picks, spread = slot_picks(ids)
    picks = jnp.concatenate(picks, axis=1)
    gates = jnp.zeros((EXPERTS, n), F32)
    for k in range(TOP):
        gates += jnp.where(ids[k : k + 1, :] == iota((EXPERTS, n), 0), given[k : k + 1, :], 0.0)
    for i in range(3):
        piece = gates.astype(BF16)
        gates = gates - piece.astype(F32)
        weight = dot(spread, piece)
        weight = jnp.concatenate([weight, weight, weight], axis=1)
        out_ref[i] = jnp.where(picks, weight, 0.0).astype(BF16)


def combine_kernel(blocks_ref, gates_ref, out_ref):
    n = out_ref.shape[1]
    blocks = blocks_ref[...]
    total = t_dot(blocks, gates_ref[0]) + t_dot(blocks, gates_ref[1]) + t_dot(blocks, gates_ref[2])
    first = total[:, :n]
    rest = total[:HLANES, n : 2 * n] + total[HLANES:, 2 * n :]
    odd = lax.axis_index("dp") % 2 == 1
    out_ref[:HLANES, :] = jnp.where(odd, rest, first[:HLANES]).astype(BF16)
    out_ref[HLANES:LANES, :] = jnp.where(odd, first[:HLANES], first[HLANES:]).astype(BF16)
    out_ref[LANES:, :] = jnp.where(odd, first[HLANES:], rest).astype(BF16)


def call(kernel, shape, *args, scratch=(), limit=16, flops=0):
    out = jax.ShapeDtypeStruct(shape, BF16) if isinstance(shape, tuple) else [pltpu.VMEM(s, d) for s, d in shape]
    sizes = sum(v.size * v.dtype.itemsize for v in args)
    return pl.pallas_call(
        kernel,
        out_shape=out,
        scratch_shapes=scratch,
        cost_estimate=pl.CostEstimate(flops=flops, transcendentals=0, bytes_accessed=sizes) if flops else None,
        compiler_params=pltpu.CompilerParams(vmem_limit_bytes=limit * 1024 * 1024),
    )(*args)


def held(value):
    return pltpu.with_memory_space_constraint(value, pltpu.VMEM)


def swap(value):
    return lax.ppermute(value, "tensor", [(0, 1), (1, 0)])


def exchange(value, axis, groups=None):
    return lax.all_to_all(value, axis, split_axis=0, concat_axis=0, tiled=True, axis_index_groups=groups)


def shards(tokens, expert_ids, gate_values, w_gate, w_up, w_down):
    n, width = tokens.shape
    plane, inside = ("dp", "tensor"), quarter_groups()
    ids, gates = expert_ids.T, gate_values.T
    own = [w_gate[0], w_up[0], w_down[0]]
    weights, down = call(
        weights_kernel, [((2 * WIDE, width), BF16), ((WIDE, width), BF16)], *own, *map(swap, own), limit=24
    )
    weights, down = held(weights), held(down)
    part_scratch = pltpu.VMEM((PART, LANES), F32)
    block_scratch = pltpu.VMEM((EXPERTS * BLOCK, LANES), F32)

    sent = call(dispatch_kernel, (EXPERTS * BLOCK, LANES), ids, tokens)
    arrived = exchange(sent.reshape(EXPERTS, BLOCK, LANES), "expert").reshape(EXPERTS * BLOCK, LANES)
    rows = call(pack_kernel, (4, PART, LANES), arrived, scratch=[block_scratch, part_scratch])
    rows = exchange(rows, plane, inside)
    others = [lax.ppermute(rows, plane, across(mask)) for mask in MASKS]
    total_shape, out_shape = ((2 * SIDE, 2 * WIDE), F32), ((4, PART, LANES), BF16)
    (total,) = call(functools.partial(first_kernel, 0), [total_shape], rows, weights, limit=32)
    for mask, other in zip(MASKS[:2], others[:2]):
        (total,) = call(functools.partial(next_kernel, mask), [total_shape], other, weights, held(total), limit=32)
    hidden, first = call(
        functools.partial(last_kernel, MASKS[2], MASKS[0]),
        [((2 * SIDE, WIDE), BF16), out_shape],
        *(others[2], weights, held(total), down),
        limit=32,
    )
    hidden = held(hidden)
    outs, work = [first], 2 * hidden.size * 8 * LANES
    for mask in (*MASKS[1:], 0):
        outs += call(functools.partial(down_kernel, mask), [out_shape], hidden, down, limit=32, flops=work)
    others = [lax.ppermute(out, plane, across(mask)) for mask, out in zip(MASKS, outs[:3])]
    partial = outs[3]
    for other, kind in zip(others, (F32, F32, BF16)):
        (partial,) = call(add_kernel, [((4, PART, LANES), kind)], held(partial), other, limit=24)
    partial = exchange(partial, plane, inside)
    summed = call(add_blocks_kernel, (EXPERTS * BLOCK, LANES), partial, scratch=[part_scratch, block_scratch])
    back = exchange(summed.reshape(EXPERTS, BLOCK, LANES), "expert").reshape(EXPERTS * BLOCK, LANES)
    (factors,) = call(gates_kernel, [((3, EXPERTS * BLOCK, 3 * n), BF16)], ids, gates)
    return call(combine_kernel, (width // DP, n), back, held(factors)).T


def solution(mesh):
    placed = (
        P(("expert", "tensor"), None),
        P("expert", None),
        P("expert", None),
        P("expert", ("dp", "tensor"), None),
        P("expert", ("dp", "tensor"), None),
        P("expert", ("dp", "tensor"), None),
    )
    return jax.shard_map(
        shards, mesh=mesh, in_specs=placed, out_specs=P(("expert", "tensor"), "dp"), check_vma=False
    )
```

```python
import functools

import jax
import jax.numpy as jnp
from jax import lax
from jax.experimental import pallas as pl
from jax.experimental.pallas import tpu as pltpu
from jax.sharding import PartitionSpec as P

EXPERTS = 16
TOP = 4
CAP = 34
HALF = CAP // 2
SIZE = 4
DP = SIZE * SIZE
LANES = 128
HLANES = 64
RISE = 40
BLOCK = 56
SIDE = EXPERTS * HALF
PART = 3 * SIDE
AWAY = ((8, 4, -4, 0), (7, -7, 1, -1), (6, -6, 2, -2), (5, -5, 3, -3))
WIDE = 384
CHUNKS = (72, 64)
MASKS = (3, 1, 2)
F32 = jnp.float32
BF16 = jnp.bfloat16


def quarter(y, x, core):
    a, b = (y + core) % SIZE, (x + core) % SIZE
    return a // 2 * 2 + b // 2, a % 2 * 2 + b % 2


def device(y, x, core):
    return (y % SIZE * SIZE + x % SIZE) * 2 + core


def quarter_groups():
    groups = {}
    for core in range(2):
        for y in range(SIZE):
            for x in range(SIZE):
                q, at = quarter(y, x, core)
                groups.setdefault((core, q), [0] * 4)[at] = device(y, x, core)
    return [groups[key] for key in sorted(groups)]


def rising(k):
    pairs = []
    for y in range(SIZE):
        for x in range(SIZE):
            for z in range(EXPERTS):
                for core in range(2):
                    to = (z + AWAY[quarter(y, x, core)[1]][k]) % EXPERTS
                    at = (y * SIZE + x) * EXPERTS
                    pairs.append(((at + z) * 2 + core, (at + to) * 2 + core))
    return pairs


def across(mask):
    pairs = []
    for core in range(2):
        for y in range(SIZE):
            for x in range(SIZE):
                up = y + 1 if (y + core) % 2 else y - 1
                right = x + 1 if (x + core) % 2 else x - 1
                pairs.append((device(y, x, core), device(up if mask & 2 else y, right if mask & 1 else x, core)))
    return pairs


def dot(a, b):
    return jnp.dot(a, b, preferred_element_type=F32)


def dot_t(a, b):
    return lax.dot_general(a, b, (((1,), (1,)), ((), ())), preferred_element_type=F32)


def t_dot(a, b):
    return lax.dot_general(a, b, (((0,), (0,)), ((), ())), preferred_element_type=F32)


def iota(shape, dim):
    return lax.broadcasted_iota(jnp.int32, shape, dim)


def slots_of(ids):
    n = ids.shape[1]
    named = jnp.zeros((EXPERTS, n), F32)
    for k in range(TOP):
        named += (ids[k : k + 1, :] == iota((EXPERTS, n), 0)).astype(F32)
    earlier = (iota((n, n), 0) < iota((n, n), 1)).astype(BF16)
    return jnp.where(named > 0.0, dot(named.astype(BF16), earlier), -1.0).astype(BF16)


def place_of():
    core, dp = lax.axis_index("tensor"), lax.axis_index("dp")
    return core, *quarter(dp // SIZE, dp % SIZE, core)


def away_of(at, k):
    away = AWAY[0][k]
    for j in range(1, 4):
        away = jnp.where(at == j, AWAY[j][k], away)
    return away


def dispatch_kernel(ids_ref, tokens_ref, *out_refs):
    n, width = tokens_ref.shape
    core, q, at = place_of()
    slots = slots_of(ids_ref[:, pl.ds(pl.multiple_of(core * n, n), n)])
    part = width // 4
    rows = tokens_ref[:, pl.ds(pl.multiple_of(q * part, part), part)]
    for k, out_ref in enumerate(out_refs):
        expert = lax.rem(lax.axis_index("expert") + away_of(at, k) + EXPERTS, EXPERTS)
        spread = (iota((RISE, EXPERTS), 1) == expert).astype(BF16)
        picks = dot(spread, slots) == iota((RISE, n), 0).astype(F32)
        out_ref[...] = dot(picks.astype(BF16), rows).astype(BF16)


def pack_kernel(*refs):
    blocks, out_refs, packed = refs[:4], refs[4:-1], refs[-1]
    for k, ref in enumerate(blocks):
        packed[k * CAP : (k + 1) * CAP, :] = ref[...].astype(F32)[:CAP]
    at = 0
    for out_ref in out_refs:
        value = packed[at : at + out_ref.shape[1], :].astype(BF16)
        at += out_ref.shape[1]
        for copy in range(out_ref.shape[0]):
            out_ref[copy] = value


def weights_kernel(gate0, up0, down0, gate1, up1, down1, weights_ref, down_ref):
    hidden, width = gate0.shape
    second = -(-hidden // 16) * 16
    for out_ref, at, pair in ((weights_ref, 0, (gate0, gate1)), (weights_ref, WIDE, (up0, up1)), (down_ref, 0, (down0, down1))):
        for start, ref, end in ((0, pair[0], second), (second, pair[1], WIDE)):
            out_ref[at + start : at + start + hidden, :] = ref[...]
            out_ref[at + start + hidden : at + end, :] = jnp.zeros((end - start - hidden, width), BF16)


def products(mask, x_ref, weights_ref):
    _, q, _ = place_of()
    part = x_ref.shape[1]
    lanes = pl.ds(pl.multiple_of((q ^ mask) * part, part), part)
    return dot_t(x_ref[...], weights_ref[:, lanes])


def down_products(mask, hidden, down_ref, out_ref):
    core, q, _ = place_of()
    to = q ^ mask
    rows = hidden.shape[0]
    side = rows // 2
    low = iota((side, LANES), 1) < HLANES
    for at in range(4):
        dp = (to // 2 * 2 + at // 2 - core) % SIZE * SIZE + (to % 2 * 2 + at % 2 - core) % SIZE
        odd = dp % 2 == 1
        y = dot(hidden, down_ref[:, pl.ds(pl.multiple_of((dp * 3 - dp % 2) // 2 * LANES, LANES), 2 * LANES)])
        first, second = y[:, :LANES], y[:, LANES:]
        out_ref[at, :rows, :] = jnp.where(odd, second, first).astype(BF16)
        half = jnp.where(odd, first, second)
        turned = pltpu.roll(half, HLANES, 1)
        left, right = jnp.where(odd, turned, half), jnp.where(odd, half, turned)
        out_ref[at, rows:, :] = jnp.where(low, left[:side], right[side:]).astype(BF16)


def first_kernel(mask, x_ref, weights_ref, total_ref):
    total_ref[...] = products(mask, x_ref, weights_ref)


def next_kernel(mask, x_ref, weights_ref, sofar_ref, total_ref):
    total_ref[...] = sofar_ref[...] + products(mask, x_ref, weights_ref)


def last_kernel(mask, x_ref, weights_ref, sofar_ref, down_ref, *out_refs):
    total = sofar_ref[...] + products(mask, x_ref, weights_ref)
    g, u = total[:, :WIDE], total[:, WIDE:]
    hidden = (g / (1.0 + jnp.exp(-g)) * u).astype(BF16)
    for to, out_ref in zip((*MASKS, 0), out_refs):
        down_products(to, hidden, down_ref, out_ref)


def add_kernel(a, b, out_ref):
    out_ref[...] = (a[...].astype(F32) + b[...].astype(F32)).astype(out_ref.dtype)


def add_blocks_kernel(*refs):
    chunks, out_ref, mains, halves, blocks = refs[: len(CHUNKS)], *refs[len(CHUNKS) :]
    start = 0
    for parts_ref, count in zip(chunks, CHUNKS):
        total = parts_ref[0].astype(F32)
        for i in range(1, parts_ref.shape[0]):
            total += parts_ref[i].astype(F32)
        for j in range(4):
            to = slice(j * 4 * CAP + start, j * 4 * CAP + start + count)
            mains[to, :] = total[j * count : (j + 1) * count]
            half = total[(4 + j % 2) * count : (5 + j % 2) * count]
            halves[to, :] = half if j < 2 else pltpu.roll(half, HLANES, 1)
        start += count
    low = iota((HALF, LANES), 1) < HLANES
    for b in range(EXPERTS):
        home = lax.rem(lax.axis_index("expert") - AWAY[b // 4][b % 4] + EXPERTS, EXPERTS)
        blocks[home, :CAP, :] = mains[b * CAP : (b + 1) * CAP, :]
        upper, lower = halves[b * CAP : b * CAP + HALF, :], halves[b * CAP + HALF : (b + 1) * CAP, :]
        blocks[home, CAP : CAP + HALF, :] = jnp.where(low, upper, pltpu.roll(lower, HLANES, 1))
        blocks[home, CAP + HALF :, :] = jnp.zeros((BLOCK - CAP - HALF, LANES), F32)
    for e in range(EXPERTS):
        out_ref[e] = blocks[e].astype(BF16)


def gates_kernel(ids_ref, gates_ref, out_ref):
    n = out_ref.shape[2] // 3
    own = pl.ds(pl.multiple_of(lax.axis_index("tensor") * n, n), n)
    ids, given = ids_ref[:, own], gates_ref[:, own]
    rows = EXPERTS * BLOCK

    def expert_of(shape):
        return jnp.floor((iota(shape, 0).astype(F32) + 0.5) * (1.0 / BLOCK))

    spread = (expert_of((rows, EXPERTS)) == iota((rows, EXPERTS), 1).astype(F32)).astype(BF16)
    wide = dot(spread, slots_of(ids))
    at = iota((rows, n), 0).astype(F32) - BLOCK * expert_of((rows, n))
    half = (at >= CAP) & (at < CAP + HALF)
    picks = jnp.concatenate(
        [(at < CAP) & (wide == at), half & (wide == at - CAP), half & (wide == at - HALF)], axis=1
    )
    gates = jnp.zeros((EXPERTS, n), F32)
    for k in range(TOP):
        gates += jnp.where(ids[k : k + 1, :] == iota((EXPERTS, n), 0), given[k : k + 1, :], 0.0)
    for i in range(3):
        piece = gates.astype(BF16)
        gates = gates - piece.astype(F32)
        weight = dot(spread, piece)
        weight = jnp.concatenate([weight, weight, weight], axis=1)
        out_ref[i] = jnp.where(picks, weight, 0.0).astype(BF16)


def combine_kernel(blocks_ref, gates_ref, out_ref):
    n = out_ref.shape[1]
    blocks = blocks_ref[...]
    total = t_dot(blocks, gates_ref[0]) + t_dot(blocks, gates_ref[1]) + t_dot(blocks, gates_ref[2])
    first = total[:, :n]
    rest = total[:HLANES, n : 2 * n] + total[HLANES:, 2 * n :]
    odd = lax.axis_index("dp") % 2 == 1
    out_ref[:HLANES, :] = jnp.where(odd, rest, first[:HLANES]).astype(BF16)
    out_ref[HLANES:LANES, :] = jnp.where(odd, first[:HLANES], first[HLANES:]).astype(BF16)
    out_ref[LANES:, :] = jnp.where(odd, first[HLANES:], rest).astype(BF16)


def call(kernel, shape, *args, scratch=(), limit=16):
    out = jax.ShapeDtypeStruct(shape, BF16) if isinstance(shape, tuple) else [pltpu.VMEM(s, d) for s, d in shape]
    return pl.pallas_call(
        kernel,
        out_shape=out,
        scratch_shapes=scratch,
        compiler_params=pltpu.CompilerParams(vmem_limit_bytes=limit * 1024 * 1024),
    )(*args)


def held(value):
    return pltpu.with_memory_space_constraint(value, pltpu.VMEM)


def swap(value):
    return lax.ppermute(value, "tensor", [(0, 1), (1, 0)])


def exchange(value, axis, groups=None):
    return lax.all_to_all(value, axis, split_axis=0, concat_axis=0, tiled=True, axis_index_groups=groups)


def shards(tokens, expert_ids, gate_values, w_gate, w_up, w_down):
    n, width = tokens.shape
    plane, inside = ("dp", "tensor"), quarter_groups()
    ids, gates = expert_ids.T, gate_values.T
    own = [w_gate[0], w_up[0], w_down[0]]
    weights, down = call(
        weights_kernel, [((2 * WIDE, width), BF16), ((WIDE, width), BF16)], *own, *map(swap, own), limit=24
    )
    weights, down = held(weights), held(down)
    part = width // 4
    sent = call(dispatch_kernel, [((RISE, part), BF16)] * 4, ids, tokens)
    arrived = [lax.ppermute(v, ("dp", "expert", "tensor"), rising(k)) for k, v in enumerate(sent)]
    rows = call(
        pack_kernel,
        [((4, count, part), BF16) for count in CHUNKS],
        *arrived,
        scratch=[pltpu.VMEM((4 * CAP, part), F32)],
    )
    rows = [exchange(chunk, plane, inside).reshape(-1, part) for chunk in rows]
    moved = [[lax.ppermute(chunk, plane, across(mask)) for mask in MASKS] for chunk in rows]
    sums = []
    for chunk, others, count in zip(rows, moved, CHUNKS):
        total_shape = [((4 * count, 2 * WIDE), F32)]
        out_shape = (4, 6 * count, LANES)
        (total,) = call(functools.partial(first_kernel, 0), total_shape, chunk, weights, limit=24)
        for mask, other in zip(MASKS[:2], others[:2]):
            (total,) = call(functools.partial(next_kernel, mask), total_shape, other, weights, held(total), limit=24)
        *outs, partial = call(
            functools.partial(last_kernel, MASKS[2]),
            [(out_shape, BF16)] * 4,
            *(others[2], weights, held(total), down),
            limit=24,
        )
        outs = [lax.ppermute(out, plane, across(mask)) for mask, out in zip(MASKS, outs)]
        for other, kind in zip(outs, (F32, F32, BF16)):
            (partial,) = call(add_kernel, [(out_shape, kind)], held(partial), other)
        sums.append(exchange(partial, plane, inside))
    summed = call(
        add_blocks_kernel,
        (EXPERTS, BLOCK, LANES),
        *sums,
        scratch=[pltpu.VMEM((2 * SIDE, LANES), F32)] * 2 + [pltpu.VMEM((EXPERTS, BLOCK, LANES), F32)],
    )
    back = exchange(summed, "expert").reshape(EXPERTS * BLOCK, LANES)
    (factors,) = call(gates_kernel, [((3, EXPERTS * BLOCK, 3 * n), BF16)], ids, gates)
    return call(combine_kernel, (width // DP, n), back, held(factors)).T


def solution(mesh):
    placed = (
        P(("expert", "tensor"), None),
        P("expert", None),
        P("expert", None),
        P("expert", ("dp", "tensor"), None),
        P("expert", ("dp", "tensor"), None),
        P("expert", ("dp", "tensor"), None),
    )
    return jax.shard_map(
        shards, mesh=mesh, in_specs=placed, out_specs=P(("expert", "tensor"), "dp"), check_vma=False
    )
```

```python
import functools

import jax
import jax.numpy as jnp
from jax import lax
from jax.experimental import pallas as pl
from jax.experimental.pallas import tpu as pltpu
from jax.sharding import PartitionSpec as P

EXPERTS = 16
TOP = 4
CAP = 34
HALF = CAP // 2
SIZE = 4
DP = SIZE * SIZE
LANES = 128
HLANES = 64
BLOCK = 56
SIDE = EXPERTS * HALF
PART = 3 * SIDE
WIDE = 384
MASKS = (3, 1, 2)
F32 = jnp.float32
BF16 = jnp.bfloat16


def quarter(y, x, core):
    a, b = (y + core) % SIZE, (x + core) % SIZE
    return a // 2 * 2 + b // 2, a % 2 * 2 + b % 2


def device(y, x, core):
    return (y % SIZE * SIZE + x % SIZE) * 2 + core


def quarter_groups():
    groups = {}
    for core in range(2):
        for y in range(SIZE):
            for x in range(SIZE):
                q, at = quarter(y, x, core)
                groups.setdefault((core, q), [0] * 4)[at] = device(y, x, core)
    return [groups[key] for key in sorted(groups)]


def across(mask):
    pairs = []
    for core in range(2):
        for y in range(SIZE):
            for x in range(SIZE):
                up = y + 1 if (y + core) % 2 else y - 1
                right = x + 1 if (x + core) % 2 else x - 1
                pairs.append((device(y, x, core), device(up if mask & 2 else y, right if mask & 1 else x, core)))
    return pairs


def dot(a, b):
    return jnp.dot(a, b, preferred_element_type=F32)


def dot_t(a, b):
    return lax.dot_general(a, b, (((1,), (1,)), ((), ())), preferred_element_type=F32)


def t_dot(a, b):
    return lax.dot_general(a, b, (((0,), (0,)), ((), ())), preferred_element_type=F32)


def iota(shape, dim):
    return lax.broadcasted_iota(jnp.int32, shape, dim)


def slot_picks(ids):
    n = ids.shape[1]
    named = jnp.zeros((EXPERTS, n), F32)
    for k in range(TOP):
        named += (ids[k : k + 1, :] == iota((EXPERTS, n), 0)).astype(F32)
    earlier = (iota((n, n), 0) < iota((n, n), 1)).astype(BF16)
    slot = jnp.where(named > 0.0, dot(named.astype(BF16), earlier), -1.0)
    rows = EXPERTS * BLOCK

    def expert_of(shape):
        return jnp.floor((iota(shape, 0).astype(F32) + 0.5) * (1.0 / BLOCK))

    spread = (expert_of((rows, EXPERTS)) == iota((rows, EXPERTS), 1).astype(F32)).astype(BF16)
    wide = dot(spread, slot.astype(BF16))
    at = iota((rows, n), 0).astype(F32) - BLOCK * expert_of((rows, n))
    main, half = at < CAP, (at >= CAP) & (at < CAP + HALF)
    return [main & (wide == at), half & (wide == at - CAP), half & (wide == at - HALF)], spread


def dispatch_kernel(ids_ref, tokens_ref, out_ref):
    n = tokens_ref.shape[0]
    core, dp = lax.axis_index("tensor"), lax.axis_index("dp")
    q, at = quarter(dp // SIZE, dp % SIZE, core)
    part = 4 * q + at
    picks, _ = slot_picks(ids_ref[:, pl.ds(pl.multiple_of(core * n, n), n)])
    picks = jnp.concatenate([p.astype(BF16) for p in picks], axis=1)
    first = tokens_ref[:, pl.ds(pl.multiple_of(part * LANES, LANES), LANES)]
    rest = tokens_ref[:, pl.ds(pl.multiple_of((DP + part // 2) * LANES, LANES), LANES)].astype(F32)
    low = iota((n, LANES), 1) < HLANES
    turned = pltpu.roll(rest, HLANES, 1)
    odd = part % 2 == 1
    here = jnp.where(odd, turned, rest)
    there = jnp.where(odd, rest, turned)
    rows = jnp.concatenate(
        [first, jnp.where(low, here, 0.0).astype(BF16), jnp.where(low, 0.0, there).astype(BF16)], axis=0
    )
    out_ref[...] = dot(picks, rows).astype(BF16)


def pack_kernel(blocks_ref, out_ref, source, packed):
    source[...] = blocks_ref[...].astype(F32)
    for e in range(EXPERTS):
        for third in range(3):
            packed[third * SIDE + e * HALF : third * SIDE + (e + 1) * HALF, :] = source[
                e * BLOCK + third * HALF : e * BLOCK + (third + 1) * HALF, :
            ]
    value = packed[...].astype(BF16)
    for copy in range(out_ref.shape[0]):
        out_ref[copy] = value


def weights_kernel(gate0, up0, down0, gate1, up1, down1, weights_ref, down_ref):
    hidden, width = gate0.shape
    second = -(-hidden // 16) * 16
    for out_ref, at, pair in ((weights_ref, 0, (gate0, gate1)), (weights_ref, WIDE, (up0, up1)), (down_ref, 0, (down0, down1))):
        for start, ref, end in ((0, pair[0], second), (second, pair[1], WIDE)):
            out_ref[at + start : at + start + hidden, :] = ref[...]
            out_ref[at + start + hidden : at + end, :] = jnp.zeros((end - start - hidden, width), BF16)


def place_of():
    core, dp = lax.axis_index("tensor"), lax.axis_index("dp")
    return core, quarter(dp // SIZE, dp % SIZE, core)[0]


def products(mask, x_ref, weights_ref):
    _, q = place_of()
    q = q ^ mask
    low = iota((SIDE, LANES), 1) < HLANES
    main = jnp.concatenate([x_ref[at, : 2 * SIDE, :] for at in range(4)], axis=1)
    halves = []
    for pair in range(2):
        even = x_ref[2 * pair, 2 * SIDE :, :].astype(F32)
        odd = x_ref[2 * pair + 1, 2 * SIDE :, :].astype(F32)
        upper = jnp.where(low, even, pltpu.roll(odd, HLANES, 1)).astype(BF16)
        lower = jnp.where(low, pltpu.roll(even, HLANES, 1), odd).astype(BF16)
        halves.append(jnp.concatenate([upper, lower], axis=0))
    rest = jnp.concatenate(halves, axis=1)
    main_lanes = pl.ds(pl.multiple_of(q * 4 * LANES, LANES), 4 * LANES)
    rest_lanes = pl.ds(pl.multiple_of((DP + q * 2) * LANES, LANES), 2 * LANES)
    return dot_t(main, weights_ref[:, main_lanes]) + dot_t(rest, weights_ref[:, rest_lanes])


def down_products(mask, hidden, down_ref, out_ref):
    core, q = place_of()
    to = q ^ mask
    low = iota((SIDE, LANES), 1) < HLANES
    for at in range(4):
        dp = (to // 2 * 2 + at // 2 - core) % SIZE * SIZE + (to % 2 * 2 + at % 2 - core) % SIZE
        odd = dp % 2 == 1
        y = dot(hidden, down_ref[:, pl.ds(pl.multiple_of((dp * 3 - dp % 2) // 2 * LANES, LANES), 2 * LANES)])
        first, second = y[:, :LANES], y[:, LANES:]
        out_ref[at, : 2 * SIDE, :] = jnp.where(odd, second, first).astype(BF16)
        half = jnp.where(odd, first, second)
        turned = pltpu.roll(half, HLANES, 1)
        left, right = jnp.where(odd, turned, half), jnp.where(odd, half, turned)
        out_ref[at, 2 * SIDE :, :] = jnp.where(low, left[:SIDE], right[SIDE:]).astype(BF16)


def first_kernel(mask, x_ref, weights_ref, total_ref):
    total_ref[...] = products(mask, x_ref, weights_ref)


def next_kernel(mask, x_ref, weights_ref, sofar_ref, total_ref):
    total_ref[...] = sofar_ref[...] + products(mask, x_ref, weights_ref)


def last_kernel(mask, x_ref, weights_ref, sofar_ref, down_ref, hidden_ref, *out_refs):
    total = sofar_ref[...] + products(mask, x_ref, weights_ref)
    g, u = total[:, :WIDE], total[:, WIDE:]
    hidden = (g / (1.0 + jnp.exp(-g)) * u).astype(BF16)
    hidden_ref[...] = hidden
    for to, out_ref in zip(MASKS, out_refs):
        down_products(to, hidden, down_ref, out_ref)


def down_kernel(mask, hidden_ref, down_ref, out_ref):
    down_products(mask, hidden_ref[...], down_ref, out_ref)


def add_kernel(a, b, out_ref):
    out_ref[...] = (a[...].astype(F32) + b[...].astype(F32)).astype(out_ref.dtype)


def add_blocks_kernel(parts_ref, out_ref, packed, blocks):
    total = parts_ref[0].astype(F32)
    for i in range(1, parts_ref.shape[0]):
        total += parts_ref[i].astype(F32)
    packed[...] = total
    for e in range(EXPERTS):
        for third in range(3):
            blocks[e * BLOCK + third * HALF : e * BLOCK + (third + 1) * HALF, :] = packed[
                third * SIDE + e * HALF : third * SIDE + (e + 1) * HALF, :
            ]
        blocks[e * BLOCK + 3 * HALF : (e + 1) * BLOCK, :] = jnp.zeros((BLOCK - 3 * HALF, LANES), F32)
    out_ref[...] = blocks[...].astype(BF16)


def gates_kernel(ids_ref, gates_ref, out_ref):
    n = out_ref.shape[2] // 3
    own = pl.ds(pl.multiple_of(lax.axis_index("tensor") * n, n), n)
    ids, given = ids_ref[:, own], gates_ref[:, own]
    picks, spread = slot_picks(ids)
    picks = jnp.concatenate(picks, axis=1)
    gates = jnp.zeros((EXPERTS, n), F32)
    for k in range(TOP):
        gates += jnp.where(ids[k : k + 1, :] == iota((EXPERTS, n), 0), given[k : k + 1, :], 0.0)
    for i in range(3):
        piece = gates.astype(BF16)
        gates = gates - piece.astype(F32)
        weight = dot(spread, piece)
        weight = jnp.concatenate([weight, weight, weight], axis=1)
        out_ref[i] = jnp.where(picks, weight, 0.0).astype(BF16)


def combine_kernel(blocks_ref, gates_ref, out_ref):
    n = out_ref.shape[1]
    blocks = blocks_ref[...]
    total = t_dot(blocks, gates_ref[0]) + t_dot(blocks, gates_ref[1]) + t_dot(blocks, gates_ref[2])
    first = total[:, :n]
    rest = total[:HLANES, n : 2 * n] + total[HLANES:, 2 * n :]
    odd = lax.axis_index("dp") % 2 == 1
    out_ref[:HLANES, :] = jnp.where(odd, rest, first[:HLANES]).astype(BF16)
    out_ref[HLANES:LANES, :] = jnp.where(odd, first[:HLANES], first[HLANES:]).astype(BF16)
    out_ref[LANES:, :] = jnp.where(odd, first[HLANES:], rest).astype(BF16)


def call(kernel, shape, *args, scratch=(), limit=16):
    out = jax.ShapeDtypeStruct(shape, BF16) if isinstance(shape, tuple) else [pltpu.VMEM(s, d) for s, d in shape]
    return pl.pallas_call(
        kernel,
        out_shape=out,
        scratch_shapes=scratch,
        compiler_params=pltpu.CompilerParams(vmem_limit_bytes=limit * 1024 * 1024),
    )(*args)


def held(value):
    return pltpu.with_memory_space_constraint(value, pltpu.VMEM)


def swap(value):
    return lax.ppermute(value, "tensor", [(0, 1), (1, 0)])


def exchange(value, axis, groups=None):
    return lax.all_to_all(value, axis, split_axis=0, concat_axis=0, tiled=True, axis_index_groups=groups)


def shards(tokens, expert_ids, gate_values, w_gate, w_up, w_down):
    n, width = tokens.shape
    plane, inside = ("dp", "tensor"), quarter_groups()
    ids, gates = expert_ids.T, gate_values.T
    own = [w_gate[0], w_up[0], w_down[0]]
    weights, down = call(
        weights_kernel, [((2 * WIDE, width), BF16), ((WIDE, width), BF16)], *own, *map(swap, own), limit=24
    )
    weights, down = held(weights), held(down)
    part_scratch = pltpu.VMEM((PART, LANES), F32)
    block_scratch = pltpu.VMEM((EXPERTS * BLOCK, LANES), F32)

    sent = call(dispatch_kernel, (EXPERTS * BLOCK, LANES), ids, tokens)
    arrived = exchange(sent.reshape(EXPERTS, BLOCK, LANES), "expert").reshape(EXPERTS * BLOCK, LANES)
    rows = call(pack_kernel, (4, PART, LANES), arrived, scratch=[block_scratch, part_scratch])
    rows = exchange(rows, plane, inside)
    others = [lax.ppermute(rows, plane, across(mask)) for mask in MASKS]
    total_shape, out_shape = ((2 * SIDE, 2 * WIDE), F32), ((4, PART, LANES), BF16)
    (total,) = call(functools.partial(first_kernel, 0), [total_shape], rows, weights, limit=32)
    for mask, other in zip(MASKS[:2], others[:2]):
        (total,) = call(functools.partial(next_kernel, mask), [total_shape], other, weights, held(total), limit=32)
    hidden, *outs = call(
        functools.partial(last_kernel, MASKS[2]),
        [((2 * SIDE, WIDE), BF16)] + [out_shape] * 3,
        *(others[2], weights, held(total), down),
        limit=32,
    )
    (partial,) = call(functools.partial(down_kernel, 0), [out_shape], held(hidden), down, limit=32)
    others = [lax.ppermute(out, plane, across(mask)) for mask, out in zip(MASKS, outs)]
    for other, kind in zip(others, (F32, F32, BF16)):
        (partial,) = call(add_kernel, [((4, PART, LANES), kind)], held(partial), other, limit=24)
    partial = exchange(partial, plane, inside)
    summed = call(add_blocks_kernel, (EXPERTS * BLOCK, LANES), partial, scratch=[part_scratch, block_scratch])
    back = exchange(summed.reshape(EXPERTS, BLOCK, LANES), "expert").reshape(EXPERTS * BLOCK, LANES)
    (factors,) = call(gates_kernel, [((3, EXPERTS * BLOCK, 3 * n), BF16)], ids, gates)
    return call(combine_kernel, (width // DP, n), back, held(factors)).T


def solution(mesh):
    placed = (
        P(("expert", "tensor"), None),
        P("expert", None),
        P("expert", None),
        P("expert", ("dp", "tensor"), None),
        P("expert", ("dp", "tensor"), None),
        P("expert", ("dp", "tensor"), None),
    )
    return jax.shard_map(
        shards, mesh=mesh, in_specs=placed, out_specs=P(("expert", "tensor"), "dp"), check_vma=False
    )
```

```python
import functools

import jax
import jax.numpy as jnp
from jax import lax
from jax.experimental import pallas as pl
from jax.experimental.pallas import tpu as pltpu
from jax.sharding import PartitionSpec as P

EXPERTS = 16
TOP = 4
CAP = 34
HALF = CAP // 2
SIZE = 4
DP = SIZE * SIZE
LANES = 128
HLANES = 64
BLOCK = 56
SIDE = EXPERTS * HALF
PART = 3 * SIDE
WIDE = 384
SIDES = (1, 2)
DIAGONAL = 3
F32 = jnp.float32
BF16 = jnp.bfloat16


def quarter(y, x, core):
    a, b = (y + core) % SIZE, (x + core) % SIZE
    return a // 2 * 2 + b // 2, a % 2 * 2 + b % 2


def device(y, x, core):
    return (y % SIZE * SIZE + x % SIZE) * 2 + core


def quarter_groups():
    groups = {}
    for core in range(2):
        for y in range(SIZE):
            for x in range(SIZE):
                q, at = quarter(y, x, core)
                groups.setdefault((core, q), [0] * 4)[at] = device(y, x, core)
    return [groups[key] for key in sorted(groups)]


def across(mask):
    pairs = []
    for core in range(2):
        for y in range(SIZE):
            for x in range(SIZE):
                up = y + 1 if (y + core) % 2 else y - 1
                right = x + 1 if (x + core) % 2 else x - 1
                pairs.append((device(y, x, core), device(up if mask & 2 else y, right if mask & 1 else x, core)))
    return pairs


def dot(a, b):
    return jnp.dot(a, b, preferred_element_type=F32)


def dot_t(a, b):
    return lax.dot_general(a, b, (((1,), (1,)), ((), ())), preferred_element_type=F32)


def t_dot(a, b):
    return lax.dot_general(a, b, (((0,), (0,)), ((), ())), preferred_element_type=F32)


def iota(shape, dim):
    return lax.broadcasted_iota(jnp.int32, shape, dim)


def slot_picks(ids):
    n = ids.shape[1]
    named = jnp.zeros((EXPERTS, n), F32)
    for k in range(TOP):
        named += (ids[k : k + 1, :] == iota((EXPERTS, n), 0)).astype(F32)
    earlier = (iota((n, n), 0) < iota((n, n), 1)).astype(BF16)
    slot = jnp.where(named > 0.0, dot(named.astype(BF16), earlier), -1.0)
    rows = EXPERTS * BLOCK

    def expert_of(shape):
        return jnp.floor((iota(shape, 0).astype(F32) + 0.5) * (1.0 / BLOCK))

    spread = (expert_of((rows, EXPERTS)) == iota((rows, EXPERTS), 1).astype(F32)).astype(BF16)
    wide = dot(spread, slot.astype(BF16))
    at = iota((rows, n), 0).astype(F32) - BLOCK * expert_of((rows, n))
    main, half = at < CAP, (at >= CAP) & (at < CAP + HALF)
    return [main & (wide == at), half & (wide == at - CAP), half & (wide == at - HALF)], spread


def dispatch_kernel(ids_ref, tokens_ref, out_ref):
    n = tokens_ref.shape[0]
    core, dp = lax.axis_index("tensor"), lax.axis_index("dp")
    q, at = quarter(dp // SIZE, dp % SIZE, core)
    part = 4 * q + at
    picks, _ = slot_picks(ids_ref[:, pl.ds(pl.multiple_of(core * n, n), n)])
    picks = jnp.concatenate([p.astype(BF16) for p in picks], axis=1)
    first = tokens_ref[:, pl.ds(pl.multiple_of(part * LANES, LANES), LANES)]
    rest = tokens_ref[:, pl.ds(pl.multiple_of((DP + part // 2) * LANES, LANES), LANES)].astype(F32)
    low = iota((n, LANES), 1) < HLANES
    turned = pltpu.roll(rest, HLANES, 1)
    odd = part % 2 == 1
    here = jnp.where(odd, turned, rest)
    there = jnp.where(odd, rest, turned)
    rows = jnp.concatenate(
        [first, jnp.where(low, here, 0.0).astype(BF16), jnp.where(low, 0.0, there).astype(BF16)], axis=0
    )
    out_ref[...] = dot(picks, rows).astype(BF16)


def pack_kernel(blocks_ref, out_ref, one_ref, source, packed):
    source[...] = blocks_ref[...].astype(F32)
    for e in range(EXPERTS):
        for third in range(3):
            packed[third * SIDE + e * HALF : third * SIDE + (e + 1) * HALF, :] = source[
                e * BLOCK + third * HALF : e * BLOCK + (third + 1) * HALF, :
            ]
    value = packed[...].astype(BF16)
    for copy in range(out_ref.shape[0]):
        out_ref[copy] = value
    one_ref[...] = value


def weights_kernel(gate0, up0, down0, gate1, up1, down1, weights_ref, down_ref):
    hidden, width = gate0.shape
    second = -(-hidden // 16) * 16
    for out_ref, at, pair in ((weights_ref, 0, (gate0, gate1)), (weights_ref, WIDE, (up0, up1)), (down_ref, 0, (down0, down1))):
        for start, ref, end in ((0, pair[0], second), (second, pair[1], WIDE)):
            out_ref[at + start : at + start + hidden, :] = ref[...]
            out_ref[at + start + hidden : at + end, :] = jnp.zeros((end - start - hidden, width), BF16)


def place_of():
    core, dp = lax.axis_index("tensor"), lax.axis_index("dp")
    return core, quarter(dp // SIZE, dp % SIZE, core)[0]


def products(mask, x_ref, weights_ref):
    _, q = place_of()
    q = q ^ mask
    turn = DIAGONAL if mask == DIAGONAL else 0
    low = iota((SIDE, LANES), 1) < HLANES
    main = jnp.concatenate([x_ref[at ^ turn, : 2 * SIDE, :] for at in range(4)], axis=1)
    halves = []
    for pair in range(2):
        even = x_ref[2 * pair ^ turn, 2 * SIDE :, :].astype(F32)
        odd = x_ref[2 * pair + 1 ^ turn, 2 * SIDE :, :].astype(F32)
        upper = jnp.where(low, even, pltpu.roll(odd, HLANES, 1)).astype(BF16)
        lower = jnp.where(low, pltpu.roll(even, HLANES, 1), odd).astype(BF16)
        halves.append(jnp.concatenate([upper, lower], axis=0))
    rest = jnp.concatenate(halves, axis=1)
    main_lanes = pl.ds(pl.multiple_of(q * 4 * LANES, LANES), 4 * LANES)
    rest_lanes = pl.ds(pl.multiple_of((DP + q * 2) * LANES, LANES), 2 * LANES)
    return dot_t(main, weights_ref[:, main_lanes]) + dot_t(rest, weights_ref[:, rest_lanes])


def down_products(mask, hidden, down_ref, out_ref):
    core, q = place_of()
    to = q ^ mask
    turn = DIAGONAL if mask == DIAGONAL else 0
    low = iota((SIDE, LANES), 1) < HLANES
    for at in range(4):
        dp = (to // 2 * 2 + at // 2 - core) % SIZE * SIZE + (to % 2 * 2 + at % 2 - core) % SIZE
        odd = dp % 2 == 1
        y = dot(hidden, down_ref[:, pl.ds(pl.multiple_of((dp * 3 - dp % 2) // 2 * LANES, LANES), 2 * LANES)])
        first, second = y[:, :LANES], y[:, LANES:]
        out_ref[at ^ turn, : 2 * SIDE, :] = jnp.where(odd, second, first).astype(BF16)
        half = jnp.where(odd, first, second)
        turned = pltpu.roll(half, HLANES, 1)
        left, right = jnp.where(odd, turned, half), jnp.where(odd, half, turned)
        out_ref[at ^ turn, 2 * SIDE :, :] = jnp.where(low, left[:SIDE], right[SIDE:]).astype(BF16)


def first_kernel(mask, x_ref, weights_ref, total_ref):
    total_ref[...] = products(mask, x_ref, weights_ref)


def next_kernel(mask, x_ref, weights_ref, sofar_ref, total_ref):
    total_ref[...] = sofar_ref[...] + products(mask, x_ref, weights_ref)


def last_kernel(mask, x_ref, weights_ref, sofar_ref, down_ref, hidden_ref, *out_refs):
    total = sofar_ref[...] + products(mask, x_ref, weights_ref)
    g, u = total[:, :WIDE], total[:, WIDE:]
    hidden = (g / (1.0 + jnp.exp(-g)) * u).astype(BF16)
    hidden_ref[...] = hidden
    for to, out_ref in zip((DIAGONAL, *SIDES), out_refs):
        down_products(to, hidden, down_ref, out_ref)


def down_kernel(mask, hidden_ref, down_ref, out_ref):
    down_products(mask, hidden_ref[...], down_ref, out_ref)


def add_kernel(a, b, out_ref):
    out_ref[...] = (a[...].astype(F32) + b[...].astype(F32)).astype(out_ref.dtype)


def add_parts_kernel(parts_ref, out_ref):
    total = parts_ref[0].astype(F32)
    for i in range(1, parts_ref.shape[0]):
        total += parts_ref[i].astype(F32)
    out_ref[...] = total.astype(BF16)


def add_blocks_kernel(parts_ref, more_ref, out_ref, packed, blocks):
    total = more_ref[...].astype(F32)
    for i in range(parts_ref.shape[0]):
        total += parts_ref[i].astype(F32)
    packed[...] = total
    for e in range(EXPERTS):
        for third in range(3):
            blocks[e * BLOCK + third * HALF : e * BLOCK + (third + 1) * HALF, :] = packed[
                third * SIDE + e * HALF : third * SIDE + (e + 1) * HALF, :
            ]
        blocks[e * BLOCK + 3 * HALF : (e + 1) * BLOCK, :] = jnp.zeros((BLOCK - 3 * HALF, LANES), F32)
    out_ref[...] = blocks[...].astype(BF16)


def gates_kernel(ids_ref, gates_ref, out_ref):
    n = out_ref.shape[2] // 3
    own = pl.ds(pl.multiple_of(lax.axis_index("tensor") * n, n), n)
    ids, given = ids_ref[:, own], gates_ref[:, own]
    picks, spread = slot_picks(ids)
    picks = jnp.concatenate(picks, axis=1)
    gates = jnp.zeros((EXPERTS, n), F32)
    for k in range(TOP):
        gates += jnp.where(ids[k : k + 1, :] == iota((EXPERTS, n), 0), given[k : k + 1, :], 0.0)
    for i in range(3):
        piece = gates.astype(BF16)
        gates = gates - piece.astype(F32)
        weight = dot(spread, piece)
        weight = jnp.concatenate([weight, weight, weight], axis=1)
        out_ref[i] = jnp.where(picks, weight, 0.0).astype(BF16)


def combine_kernel(blocks_ref, gates_ref, out_ref):
    n = out_ref.shape[1]
    blocks = blocks_ref[...]
    total = t_dot(blocks, gates_ref[0]) + t_dot(blocks, gates_ref[1]) + t_dot(blocks, gates_ref[2])
    first = total[:, :n]
    rest = total[:HLANES, n : 2 * n] + total[HLANES:, 2 * n :]
    odd = lax.axis_index("dp") % 2 == 1
    out_ref[:HLANES, :] = jnp.where(odd, rest, first[:HLANES]).astype(BF16)
    out_ref[HLANES:LANES, :] = jnp.where(odd, first[:HLANES], first[HLANES:]).astype(BF16)
    out_ref[LANES:, :] = jnp.where(odd, first[HLANES:], rest).astype(BF16)


def call(kernel, shape, *args, scratch=(), limit=16):
    out = jax.ShapeDtypeStruct(shape, BF16) if isinstance(shape, tuple) else [pltpu.VMEM(s, d) for s, d in shape]
    return pl.pallas_call(
        kernel,
        out_shape=out,
        scratch_shapes=scratch,
        compiler_params=pltpu.CompilerParams(vmem_limit_bytes=limit * 1024 * 1024),
    )(*args)


def held(value):
    return pltpu.with_memory_space_constraint(value, pltpu.VMEM)


def swap(value):
    return lax.ppermute(value, "tensor", [(0, 1), (1, 0)])


def exchange(value, axis, groups=None):
    return lax.all_to_all(value, axis, split_axis=0, concat_axis=0, tiled=True, axis_index_groups=groups)


def shards(tokens, expert_ids, gate_values, w_gate, w_up, w_down):
    n, width = tokens.shape
    plane, inside = ("dp", "tensor"), quarter_groups()
    ids, gates = expert_ids.T, gate_values.T
    own = [w_gate[0], w_up[0], w_down[0]]
    weights, down = call(
        weights_kernel, [((2 * WIDE, width), BF16), ((WIDE, width), BF16)], *own, *map(swap, own), limit=24
    )
    weights, down = held(weights), held(down)
    part_scratch = pltpu.VMEM((PART, LANES), F32)
    block_scratch = pltpu.VMEM((EXPERTS * BLOCK, LANES), F32)

    sent = call(dispatch_kernel, (EXPERTS * BLOCK, LANES), ids, tokens)
    arrived = exchange(sent.reshape(EXPERTS, BLOCK, LANES), "expert").reshape(EXPERTS * BLOCK, LANES)
    out_shape = (4, PART, LANES)
    rows, one = call(
        pack_kernel, [(out_shape, BF16), (out_shape[1:], BF16)], arrived, scratch=[block_scratch, part_scratch]
    )
    rows = exchange(rows, plane, inside)
    one = lax.ppermute(one, plane, across(DIAGONAL))
    others = [lax.ppermute(rows, plane, across(mask)) for mask in SIDES]
    diagonal = exchange(jnp.broadcast_to(one, out_shape), plane, inside)
    total_shape = [((2 * SIDE, 2 * WIDE), F32)]
    (total,) = call(functools.partial(first_kernel, 0), total_shape, rows, weights, limit=32)
    for mask, other in zip(SIDES, others):
        (total,) = call(functools.partial(next_kernel, mask), total_shape, other, weights, held(total), limit=32)
    hidden, across_out, *outs = call(
        functools.partial(last_kernel, DIAGONAL),
        [((2 * SIDE, WIDE), BF16)] + [(out_shape, BF16)] * 3,
        *(diagonal, weights, held(total), down),
        limit=32,
    )
    (partial,) = call(functools.partial(down_kernel, 0), [(out_shape, BF16)], held(hidden), down, limit=32)
    others = [lax.ppermute(out, plane, across(mask)) for mask, out in zip(SIDES, outs)]
    one = call(add_parts_kernel, out_shape[1:], exchange(across_out, plane, inside))
    one = lax.ppermute(one, plane, across(DIAGONAL))
    for other, kind in zip(others, (F32, BF16)):
        (partial,) = call(add_kernel, [(out_shape, kind)], held(partial), other, limit=24)
    partial = exchange(partial, plane, inside)
    summed = call(
        add_blocks_kernel, (EXPERTS * BLOCK, LANES), partial, one, scratch=[part_scratch, block_scratch]
    ).reshape(EXPERTS, BLOCK, LANES)
    back = exchange(summed, "expert").reshape(EXPERTS * BLOCK, LANES)
    (factors,) = call(gates_kernel, [((3, EXPERTS * BLOCK, 3 * n), BF16)], ids, gates)
    return call(combine_kernel, (width // DP, n), back, held(factors)).T


def solution(mesh):
    placed = (
        P(("expert", "tensor"), None),
        P("expert", None),
        P("expert", None),
        P("expert", ("dp", "tensor"), None),
        P("expert", ("dp", "tensor"), None),
        P("expert", ("dp", "tensor"), None),
    )
    return jax.shard_map(
        shards, mesh=mesh, in_specs=placed, out_specs=P(("expert", "tensor"), "dp"), check_vma=False
    )
```

```python
import functools

import jax
import jax.numpy as jnp
from jax import lax
from jax.experimental import pallas as pl
from jax.experimental.pallas import tpu as pltpu
from jax.sharding import PartitionSpec as P

EXPERTS = 16
TOP = 4
CAP = 34
HALF = CAP // 2
SIZE = 4
DP = SIZE * SIZE
LANES = 128
HLANES = 64
BLOCK = 56
SIDE = EXPERTS * HALF
PART = 3 * SIDE
WIDE = 384
MASKS = (3, 1, 2)
F32 = jnp.float32
BF16 = jnp.bfloat16


def quarter(y, x, cut):
    a, b = (y + cut) % SIZE, (x + cut) % SIZE
    return a // 2 * 2 + b // 2, a % 2 * 2 + b % 2


def device(y, x, core):
    return (y % SIZE * SIZE + x % SIZE) * 2 + core


def quarter_groups(back):
    groups = {}
    for core in range(2):
        for y in range(SIZE):
            for x in range(SIZE):
                q, at = quarter(y, x, core ^ back)
                groups.setdefault((core, q), [0] * 4)[at] = device(y, x, core)
    return [groups[key] for key in sorted(groups)]


def across(mask, back):
    pairs = []
    for core in range(2):
        cut = core ^ back
        for y in range(SIZE):
            for x in range(SIZE):
                up = y + 1 if (y + cut) % 2 else y - 1
                right = x + 1 if (x + cut) % 2 else x - 1
                pairs.append((device(y, x, core), device(up if mask & 2 else y, right if mask & 1 else x, core)))
    return pairs


def dot(a, b):
    return jnp.dot(a, b, preferred_element_type=F32)


def dot_t(a, b):
    return lax.dot_general(a, b, (((1,), (1,)), ((), ())), preferred_element_type=F32)


def t_dot(a, b):
    return lax.dot_general(a, b, (((0,), (0,)), ((), ())), preferred_element_type=F32)


def iota(shape, dim):
    return lax.broadcasted_iota(jnp.int32, shape, dim)


def slot_picks(ids):
    n = ids.shape[1]
    named = jnp.zeros((EXPERTS, n), F32)
    for k in range(TOP):
        named += (ids[k : k + 1, :] == iota((EXPERTS, n), 0)).astype(F32)
    earlier = (iota((n, n), 0) < iota((n, n), 1)).astype(BF16)
    slot = jnp.where(named > 0.0, dot(named.astype(BF16), earlier), -1.0)
    rows = EXPERTS * BLOCK

    def expert_of(shape):
        return jnp.floor((iota(shape, 0).astype(F32) + 0.5) * (1.0 / BLOCK))

    spread = (expert_of((rows, EXPERTS)) == iota((rows, EXPERTS), 1).astype(F32)).astype(BF16)
    wide = dot(spread, slot.astype(BF16))
    at = iota((rows, n), 0).astype(F32) - BLOCK * expert_of((rows, n))
    main, half = at < CAP, (at >= CAP) & (at < CAP + HALF)
    return [main & (wide == at), half & (wide == at - CAP), half & (wide == at - HALF)], spread


def dispatch_kernel(ids_ref, tokens_ref, out_ref):
    n = tokens_ref.shape[0]
    core, dp = lax.axis_index("tensor"), lax.axis_index("dp")
    q, at = quarter(dp // SIZE, dp % SIZE, core)
    part = 4 * q + at
    picks, _ = slot_picks(ids_ref[:, pl.ds(pl.multiple_of(core * n, n), n)])
    picks = jnp.concatenate([p.astype(BF16) for p in picks], axis=1)
    first = tokens_ref[:, pl.ds(pl.multiple_of(part * LANES, LANES), LANES)]
    rest = tokens_ref[:, pl.ds(pl.multiple_of((DP + part // 2) * LANES, LANES), LANES)].astype(F32)
    low = iota((n, LANES), 1) < HLANES
    turned = pltpu.roll(rest, HLANES, 1)
    odd = part % 2 == 1
    here = jnp.where(odd, turned, rest)
    there = jnp.where(odd, rest, turned)
    rows = jnp.concatenate(
        [first, jnp.where(low, here, 0.0).astype(BF16), jnp.where(low, 0.0, there).astype(BF16)], axis=0
    )
    out_ref[...] = dot(picks, rows).astype(BF16)


def pack_kernel(blocks_ref, out_ref, source, packed):
    source[...] = blocks_ref[...].astype(F32)
    for e in range(EXPERTS):
        for third in range(3):
            packed[third * SIDE + e * HALF : third * SIDE + (e + 1) * HALF, :] = source[
                e * BLOCK + third * HALF : e * BLOCK + (third + 1) * HALF, :
            ]
    value = packed[...].astype(BF16)
    for copy in range(out_ref.shape[0]):
        out_ref[copy] = value


def weights_kernel(gate0, up0, down0, gate1, up1, down1, weights_ref, down_ref):
    hidden, width = gate0.shape
    second = -(-hidden // 16) * 16
    for out_ref, at, pair in ((weights_ref, 0, (gate0, gate1)), (weights_ref, WIDE, (up0, up1)), (down_ref, 0, (down0, down1))):
        for start, ref, end in ((0, pair[0], second), (second, pair[1], WIDE)):
            out_ref[at + start : at + start + hidden, :] = ref[...]
            out_ref[at + start + hidden : at + end, :] = jnp.zeros((end - start - hidden, width), BF16)


def place_of(back):
    cut, dp = lax.axis_index("tensor") ^ back, lax.axis_index("dp")
    return cut, quarter(dp // SIZE, dp % SIZE, cut)[0]


def products(mask, x_ref, weights_ref):
    _, q = place_of(0)
    q = q ^ mask
    low = iota((SIDE, LANES), 1) < HLANES
    main = jnp.concatenate([x_ref[at, : 2 * SIDE, :] for at in range(4)], axis=1)
    halves = []
    for pair in range(2):
        even = x_ref[2 * pair, 2 * SIDE :, :].astype(F32)
        odd = x_ref[2 * pair + 1, 2 * SIDE :, :].astype(F32)
        upper = jnp.where(low, even, pltpu.roll(odd, HLANES, 1)).astype(BF16)
        lower = jnp.where(low, pltpu.roll(even, HLANES, 1), odd).astype(BF16)
        halves.append(jnp.concatenate([upper, lower], axis=0))
    rest = jnp.concatenate(halves, axis=1)
    main_lanes = pl.ds(pl.multiple_of(q * 4 * LANES, LANES), 4 * LANES)
    rest_lanes = pl.ds(pl.multiple_of((DP + q * 2) * LANES, LANES), 2 * LANES)
    return dot_t(main, weights_ref[:, main_lanes]) + dot_t(rest, weights_ref[:, rest_lanes])


def down_products(mask, hidden, down_ref, out_ref):
    cut, q = place_of(1)
    to = q ^ mask
    low = iota((SIDE, LANES), 1) < HLANES
    for at in range(4):
        dp = (to // 2 * 2 + at // 2 - cut) % SIZE * SIZE + (to % 2 * 2 + at % 2 - cut) % SIZE
        odd = dp % 2 == 1
        y = dot(hidden, down_ref[:, pl.ds(pl.multiple_of((dp * 3 - dp % 2) // 2 * LANES, LANES), 2 * LANES)])
        first, second = y[:, :LANES], y[:, LANES:]
        out_ref[at, : 2 * SIDE, :] = jnp.where(odd, second, first).astype(BF16)
        half = jnp.where(odd, first, second)
        turned = pltpu.roll(half, HLANES, 1)
        left, right = jnp.where(odd, turned, half), jnp.where(odd, half, turned)
        out_ref[at, 2 * SIDE :, :] = jnp.where(low, left[:SIDE], right[SIDE:]).astype(BF16)


def first_kernel(mask, x_ref, weights_ref, total_ref):
    total_ref[...] = products(mask, x_ref, weights_ref)


def next_kernel(mask, x_ref, weights_ref, sofar_ref, total_ref):
    total_ref[...] = sofar_ref[...] + products(mask, x_ref, weights_ref)


def last_kernel(mask, x_ref, weights_ref, sofar_ref, down_ref, hidden_ref, *out_refs):
    total = sofar_ref[...] + products(mask, x_ref, weights_ref)
    g, u = total[:, :WIDE], total[:, WIDE:]
    hidden = (g / (1.0 + jnp.exp(-g)) * u).astype(BF16)
    hidden_ref[...] = hidden
    for to, out_ref in zip(MASKS, out_refs):
        down_products(to, hidden, down_ref, out_ref)


def down_kernel(mask, hidden_ref, down_ref, out_ref):
    down_products(mask, hidden_ref[...], down_ref, out_ref)


def add_kernel(a, b, out_ref):
    out_ref[...] = (a[...].astype(F32) + b[...].astype(F32)).astype(out_ref.dtype)


def add_blocks_kernel(parts_ref, out_ref, packed, blocks):
    total = parts_ref[0].astype(F32)
    for i in range(1, parts_ref.shape[0]):
        total += parts_ref[i].astype(F32)
    packed[...] = total
    for e in range(EXPERTS):
        for third in range(3):
            blocks[e * BLOCK + third * HALF : e * BLOCK + (third + 1) * HALF, :] = packed[
                third * SIDE + e * HALF : third * SIDE + (e + 1) * HALF, :
            ]
        blocks[e * BLOCK + 3 * HALF : (e + 1) * BLOCK, :] = jnp.zeros((BLOCK - 3 * HALF, LANES), F32)
    out_ref[...] = blocks[...].astype(BF16)


def gates_kernel(ids_ref, gates_ref, out_ref):
    n = out_ref.shape[2] // 3
    own = pl.ds(pl.multiple_of(lax.axis_index("tensor") * n, n), n)
    ids, given = ids_ref[:, own], gates_ref[:, own]
    picks, spread = slot_picks(ids)
    picks = jnp.concatenate(picks, axis=1)
    gates = jnp.zeros((EXPERTS, n), F32)
    for k in range(TOP):
        gates += jnp.where(ids[k : k + 1, :] == iota((EXPERTS, n), 0), given[k : k + 1, :], 0.0)
    for i in range(3):
        piece = gates.astype(BF16)
        gates = gates - piece.astype(F32)
        weight = dot(spread, piece)
        weight = jnp.concatenate([weight, weight, weight], axis=1)
        out_ref[i] = jnp.where(picks, weight, 0.0).astype(BF16)


def combine_kernel(blocks_ref, gates_ref, out_ref):
    n = out_ref.shape[1]
    blocks = blocks_ref[...]
    total = t_dot(blocks, gates_ref[0]) + t_dot(blocks, gates_ref[1]) + t_dot(blocks, gates_ref[2])
    first = total[:, :n]
    rest = total[:HLANES, n : 2 * n] + total[HLANES:, 2 * n :]
    odd = lax.axis_index("dp") % 2 == 1
    out_ref[:HLANES, :] = jnp.where(odd, rest, first[:HLANES]).astype(BF16)
    out_ref[HLANES:LANES, :] = jnp.where(odd, first[:HLANES], first[HLANES:]).astype(BF16)
    out_ref[LANES:, :] = jnp.where(odd, first[HLANES:], rest).astype(BF16)


def call(kernel, shape, *args, scratch=(), limit=16):
    out = jax.ShapeDtypeStruct(shape, BF16) if isinstance(shape, tuple) else [pltpu.VMEM(s, d) for s, d in shape]
    return pl.pallas_call(
        kernel,
        out_shape=out,
        scratch_shapes=scratch,
        compiler_params=pltpu.CompilerParams(vmem_limit_bytes=limit * 1024 * 1024),
    )(*args)


def held(value):
    return pltpu.with_memory_space_constraint(value, pltpu.VMEM)


def swap(value):
    return lax.ppermute(value, "tensor", [(0, 1), (1, 0)])


def exchange(value, axis, groups=None):
    return lax.all_to_all(value, axis, split_axis=0, concat_axis=0, tiled=True, axis_index_groups=groups)


def shards(tokens, expert_ids, gate_values, w_gate, w_up, w_down):
    n, width = tokens.shape
    plane = ("dp", "tensor")
    ids, gates = expert_ids.T, gate_values.T
    own = [w_gate[0], w_up[0], w_down[0]]
    weights, down = call(
        weights_kernel, [((2 * WIDE, width), BF16), ((WIDE, width), BF16)], *own, *map(swap, own), limit=24
    )
    weights, down = held(weights), held(down)
    part_scratch = pltpu.VMEM((PART, LANES), F32)
    block_scratch = pltpu.VMEM((EXPERTS * BLOCK, LANES), F32)

    sent = call(dispatch_kernel, (EXPERTS * BLOCK, LANES), ids, tokens)
    arrived = exchange(sent.reshape(EXPERTS, BLOCK, LANES), "expert").reshape(EXPERTS * BLOCK, LANES)
    rows = call(pack_kernel, (4, PART, LANES), arrived, scratch=[block_scratch, part_scratch])
    rows = exchange(rows, plane, quarter_groups(0))
    others = [lax.ppermute(rows, plane, across(mask, 0)) for mask in MASKS]
    total_shape, out_shape = ((2 * SIDE, 2 * WIDE), F32), ((4, PART, LANES), BF16)
    (total,) = call(functools.partial(first_kernel, 0), [total_shape], rows, weights, limit=32)
    for mask, other in zip(MASKS[:2], others[:2]):
        (total,) = call(functools.partial(next_kernel, mask), [total_shape], other, weights, held(total), limit=32)
    hidden, *outs = call(
        functools.partial(last_kernel, MASKS[2]),
        [((2 * SIDE, WIDE), BF16)] + [out_shape] * 3,
        *(others[2], weights, held(total), down),
        limit=32,
    )
    (partial,) = call(functools.partial(down_kernel, 0), [out_shape], held(hidden), down, limit=32)
    others = [lax.ppermute(out, plane, across(mask, 1)) for mask, out in zip(MASKS, outs)]
    for other, kind in zip(others, (F32, F32, BF16)):
        (partial,) = call(add_kernel, [((4, PART, LANES), kind)], held(partial), other, limit=24)
    partial = exchange(partial, plane, quarter_groups(1))
    summed = call(add_blocks_kernel, (EXPERTS * BLOCK, LANES), partial, scratch=[part_scratch, block_scratch])
    back = exchange(summed.reshape(EXPERTS, BLOCK, LANES), "expert").reshape(EXPERTS * BLOCK, LANES)
    (factors,) = call(gates_kernel, [((3, EXPERTS * BLOCK, 3 * n), BF16)], ids, gates)
    return call(combine_kernel, (width // DP, n), back, held(factors)).T


def solution(mesh):
    placed = (
        P(("expert", "tensor"), None),
        P("expert", None),
        P("expert", None),
        P("expert", ("dp", "tensor"), None),
        P("expert", ("dp", "tensor"), None),
        P("expert", ("dp", "tensor"), None),
    )
    return jax.shard_map(
        shards, mesh=mesh, in_specs=placed, out_specs=P(("expert", "tensor"), "dp"), check_vma=False
    )
```

```python
import functools

import jax
import jax.numpy as jnp
from jax import lax
from jax.experimental import pallas as pl
from jax.experimental.pallas import tpu as pltpu
from jax.sharding import PartitionSpec as P

EXPERTS = 16
TOP = 4
CAP = 34
HALF = CAP // 2
SIZE = 4
DP = SIZE * SIZE
LANES = 128
HLANES = 64
BLOCK = 56
SIDE = EXPERTS * HALF
PART = 3 * SIDE
WIDE = 384
MASKS = (3, 1, 2)
F32 = jnp.float32
BF16 = jnp.bfloat16


def quarter(y, x, cut):
    a, b = (y + cut) % SIZE, (x + cut) % SIZE
    return a // 2 * 2 + b // 2, a % 2 * 2 + b % 2


def device(y, x, core):
    return (y % SIZE * SIZE + x % SIZE) * 2 + core


def quarter_groups():
    groups = {}
    for core in range(2):
        for y in range(SIZE):
            for x in range(SIZE):
                q, at = quarter(y, x, 1 - core)
                groups.setdefault((core, q), [0] * 4)[at] = device(y, x, core)
    return [groups[key] for key in sorted(groups)]


def across(mask):
    pairs = []
    for core in range(2):
        cut = 1 - core
        for y in range(SIZE):
            for x in range(SIZE):
                up = y + 1 if (y + cut) % 2 else y - 1
                right = x + 1 if (x + cut) % 2 else x - 1
                pairs.append((device(y, x, core), device(up if mask & 2 else y, right if mask & 1 else x, core)))
    return pairs


def dot(a, b):
    return jnp.dot(a, b, preferred_element_type=F32)


def dot_t(a, b):
    return lax.dot_general(a, b, (((1,), (1,)), ((), ())), preferred_element_type=F32)


def t_dot(a, b):
    return lax.dot_general(a, b, (((0,), (0,)), ((), ())), preferred_element_type=F32)


def iota(shape, dim):
    return lax.broadcasted_iota(jnp.int32, shape, dim)


def slot_picks(ids):
    n = ids.shape[1]
    named = jnp.zeros((EXPERTS, n), F32)
    for k in range(TOP):
        named += (ids[k : k + 1, :] == iota((EXPERTS, n), 0)).astype(F32)
    earlier = (iota((n, n), 0) < iota((n, n), 1)).astype(BF16)
    slot = jnp.where(named > 0.0, dot(named.astype(BF16), earlier), -1.0)
    rows = EXPERTS * BLOCK

    def expert_of(shape):
        return jnp.floor((iota(shape, 0).astype(F32) + 0.5) * (1.0 / BLOCK))

    spread = (expert_of((rows, EXPERTS)) == iota((rows, EXPERTS), 1).astype(F32)).astype(BF16)
    wide = dot(spread, slot.astype(BF16))
    at = iota((rows, n), 0).astype(F32) - BLOCK * expert_of((rows, n))
    main, half = at < CAP, (at >= CAP) & (at < CAP + HALF)
    return [main & (wide == at), half & (wide == at - CAP), half & (wide == at - HALF)], spread


def dispatch_kernel(ids_ref, tokens_ref, out_ref):
    n = tokens_ref.shape[0]
    core, dp = lax.axis_index("tensor"), lax.axis_index("dp")
    q, at = quarter(dp // SIZE, dp % SIZE, 1 - core)
    part = 4 * q + at
    picks, _ = slot_picks(ids_ref[:, pl.ds(pl.multiple_of(core * n, n), n)])
    picks = jnp.concatenate([p.astype(BF16) for p in picks], axis=1)
    first = tokens_ref[:, pl.ds(pl.multiple_of(part * LANES, LANES), LANES)]
    rest = tokens_ref[:, pl.ds(pl.multiple_of((DP + part // 2) * LANES, LANES), LANES)].astype(F32)
    low = iota((n, LANES), 1) < HLANES
    turned = pltpu.roll(rest, HLANES, 1)
    odd = part % 2 == 1
    here = jnp.where(odd, turned, rest)
    there = jnp.where(odd, rest, turned)
    rows = jnp.concatenate(
        [first, jnp.where(low, here, 0.0).astype(BF16), jnp.where(low, 0.0, there).astype(BF16)], axis=0
    )
    out_ref[...] = dot(picks, rows).astype(BF16)


def pack_kernel(blocks_ref, out_ref, source, packed):
    source[...] = blocks_ref[...].astype(F32)
    for e in range(EXPERTS):
        for third in range(3):
            packed[third * SIDE + e * HALF : third * SIDE + (e + 1) * HALF, :] = source[
                e * BLOCK + third * HALF : e * BLOCK + (third + 1) * HALF, :
            ]
    value = packed[...].astype(BF16)
    for copy in range(out_ref.shape[0]):
        out_ref[copy] = value


def weights_kernel(gate0, up0, down0, gate1, up1, down1, weights_ref, down_ref):
    hidden, width = gate0.shape
    second = -(-hidden // 16) * 16
    for out_ref, at, pair in ((weights_ref, 0, (gate0, gate1)), (weights_ref, WIDE, (up0, up1)), (down_ref, 0, (down0, down1))):
        for start, ref, end in ((0, pair[0], second), (second, pair[1], WIDE)):
            out_ref[at + start : at + start + hidden, :] = ref[...]
            out_ref[at + start + hidden : at + end, :] = jnp.zeros((end - start - hidden, width), BF16)


def place_of():
    cut, dp = 1 - lax.axis_index("tensor"), lax.axis_index("dp")
    return cut, quarter(dp // SIZE, dp % SIZE, cut)[0]


def products(mask, x_ref, weights_ref):
    _, q = place_of()
    q = q ^ mask
    low = iota((SIDE, LANES), 1) < HLANES
    main = jnp.concatenate([x_ref[at, : 2 * SIDE, :] for at in range(4)], axis=1)
    halves = []
    for pair in range(2):
        even = x_ref[2 * pair, 2 * SIDE :, :].astype(F32)
        odd = x_ref[2 * pair + 1, 2 * SIDE :, :].astype(F32)
        upper = jnp.where(low, even, pltpu.roll(odd, HLANES, 1)).astype(BF16)
        lower = jnp.where(low, pltpu.roll(even, HLANES, 1), odd).astype(BF16)
        halves.append(jnp.concatenate([upper, lower], axis=0))
    rest = jnp.concatenate(halves, axis=1)
    main_lanes = pl.ds(pl.multiple_of(q * 4 * LANES, LANES), 4 * LANES)
    rest_lanes = pl.ds(pl.multiple_of((DP + q * 2) * LANES, LANES), 2 * LANES)
    return dot_t(main, weights_ref[:, main_lanes]) + dot_t(rest, weights_ref[:, rest_lanes])


def down_products(mask, hidden, down_ref, out_ref):
    cut, q = place_of()
    to = q ^ mask
    low = iota((SIDE, LANES), 1) < HLANES
    for at in range(4):
        dp = (to // 2 * 2 + at // 2 - cut) % SIZE * SIZE + (to % 2 * 2 + at % 2 - cut) % SIZE
        odd = dp % 2 == 1
        y = dot(hidden, down_ref[:, pl.ds(pl.multiple_of((dp * 3 - dp % 2) // 2 * LANES, LANES), 2 * LANES)])
        first, second = y[:, :LANES], y[:, LANES:]
        out_ref[at, : 2 * SIDE, :] = jnp.where(odd, second, first).astype(BF16)
        half = jnp.where(odd, first, second)
        turned = pltpu.roll(half, HLANES, 1)
        left, right = jnp.where(odd, turned, half), jnp.where(odd, half, turned)
        out_ref[at, 2 * SIDE :, :] = jnp.where(low, left[:SIDE], right[SIDE:]).astype(BF16)


def first_kernel(mask, x_ref, weights_ref, total_ref):
    total_ref[...] = products(mask, x_ref, weights_ref)


def next_kernel(mask, x_ref, weights_ref, sofar_ref, total_ref):
    total_ref[...] = sofar_ref[...] + products(mask, x_ref, weights_ref)


def last_kernel(mask, x_ref, weights_ref, sofar_ref, down_ref, hidden_ref, *out_refs):
    total = sofar_ref[...] + products(mask, x_ref, weights_ref)
    g, u = total[:, :WIDE], total[:, WIDE:]
    hidden = (g / (1.0 + jnp.exp(-g)) * u).astype(BF16)
    hidden_ref[...] = hidden
    for to, out_ref in zip(MASKS, out_refs):
        down_products(to, hidden, down_ref, out_ref)


def down_kernel(mask, hidden_ref, down_ref, out_ref):
    down_products(mask, hidden_ref[...], down_ref, out_ref)


def add_kernel(a, b, out_ref):
    out_ref[...] = (a[...].astype(F32) + b[...].astype(F32)).astype(out_ref.dtype)


def add_blocks_kernel(parts_ref, out_ref, packed, blocks):
    total = parts_ref[0].astype(F32)
    for i in range(1, parts_ref.shape[0]):
        total += parts_ref[i].astype(F32)
    packed[...] = total
    for e in range(EXPERTS):
        for third in range(3):
            blocks[e * BLOCK + third * HALF : e * BLOCK + (third + 1) * HALF, :] = packed[
                third * SIDE + e * HALF : third * SIDE + (e + 1) * HALF, :
            ]
        blocks[e * BLOCK + 3 * HALF : (e + 1) * BLOCK, :] = jnp.zeros((BLOCK - 3 * HALF, LANES), F32)
    out_ref[...] = blocks[...].astype(BF16)


def gates_kernel(ids_ref, gates_ref, out_ref):
    n = out_ref.shape[2] // 3
    own = pl.ds(pl.multiple_of(lax.axis_index("tensor") * n, n), n)
    ids, given = ids_ref[:, own], gates_ref[:, own]
    picks, spread = slot_picks(ids)
    picks = jnp.concatenate(picks, axis=1)
    gates = jnp.zeros((EXPERTS, n), F32)
    for k in range(TOP):
        gates += jnp.where(ids[k : k + 1, :] == iota((EXPERTS, n), 0), given[k : k + 1, :], 0.0)
    for i in range(3):
        piece = gates.astype(BF16)
        gates = gates - piece.astype(F32)
        weight = dot(spread, piece)
        weight = jnp.concatenate([weight, weight, weight], axis=1)
        out_ref[i] = jnp.where(picks, weight, 0.0).astype(BF16)


def combine_kernel(blocks_ref, gates_ref, out_ref):
    n = out_ref.shape[1]
    blocks = blocks_ref[...]
    total = t_dot(blocks, gates_ref[0]) + t_dot(blocks, gates_ref[1]) + t_dot(blocks, gates_ref[2])
    first = total[:, :n]
    rest = total[:HLANES, n : 2 * n] + total[HLANES:, 2 * n :]
    odd = lax.axis_index("dp") % 2 == 1
    out_ref[:HLANES, :] = jnp.where(odd, rest, first[:HLANES]).astype(BF16)
    out_ref[HLANES:LANES, :] = jnp.where(odd, first[:HLANES], first[HLANES:]).astype(BF16)
    out_ref[LANES:, :] = jnp.where(odd, first[HLANES:], rest).astype(BF16)


def call(kernel, shape, *args, scratch=(), limit=16):
    out = jax.ShapeDtypeStruct(shape, BF16) if isinstance(shape, tuple) else [pltpu.VMEM(s, d) for s, d in shape]
    return pl.pallas_call(
        kernel,
        out_shape=out,
        scratch_shapes=scratch,
        compiler_params=pltpu.CompilerParams(vmem_limit_bytes=limit * 1024 * 1024),
    )(*args)


def held(value):
    return pltpu.with_memory_space_constraint(value, pltpu.VMEM)


def swap(value):
    return lax.ppermute(value, "tensor", [(0, 1), (1, 0)])


def exchange(value, axis, groups=None):
    return lax.all_to_all(value, axis, split_axis=0, concat_axis=0, tiled=True, axis_index_groups=groups)


def shards(tokens, expert_ids, gate_values, w_gate, w_up, w_down):
    n, width = tokens.shape
    plane = ("dp", "tensor")
    ids, gates = expert_ids.T, gate_values.T
    own = [w_gate[0], w_up[0], w_down[0]]
    weights, down = call(
        weights_kernel, [((2 * WIDE, width), BF16), ((WIDE, width), BF16)], *own, *map(swap, own), limit=24
    )
    weights, down = held(weights), held(down)
    part_scratch = pltpu.VMEM((PART, LANES), F32)
    block_scratch = pltpu.VMEM((EXPERTS * BLOCK, LANES), F32)

    sent = call(dispatch_kernel, (EXPERTS * BLOCK, LANES), ids, tokens)
    arrived = exchange(sent.reshape(EXPERTS, BLOCK, LANES), "expert").reshape(EXPERTS * BLOCK, LANES)
    rows = call(pack_kernel, (4, PART, LANES), arrived, scratch=[block_scratch, part_scratch])
    rows = exchange(rows, plane, quarter_groups())
    others = [lax.ppermute(rows, plane, across(mask)) for mask in MASKS]
    total_shape, out_shape = ((2 * SIDE, 2 * WIDE), F32), ((4, PART, LANES), BF16)
    (total,) = call(functools.partial(first_kernel, 0), [total_shape], rows, weights, limit=32)
    for mask, other in zip(MASKS[:2], others[:2]):
        (total,) = call(functools.partial(next_kernel, mask), [total_shape], other, weights, held(total), limit=32)
    hidden, *outs = call(
        functools.partial(last_kernel, MASKS[2]),
        [((2 * SIDE, WIDE), BF16)] + [out_shape] * 3,
        *(others[2], weights, held(total), down),
        limit=32,
    )
    (partial,) = call(functools.partial(down_kernel, 0), [out_shape], held(hidden), down, limit=32)
    others = [lax.ppermute(out, plane, across(mask)) for mask, out in zip(MASKS, outs)]
    for other, kind in zip(others, (F32, F32, BF16)):
        (partial,) = call(add_kernel, [((4, PART, LANES), kind)], held(partial), other, limit=24)
    partial = exchange(partial, plane, quarter_groups())
    summed = call(add_blocks_kernel, (EXPERTS * BLOCK, LANES), partial, scratch=[part_scratch, block_scratch])
    back = exchange(summed.reshape(EXPERTS, BLOCK, LANES), "expert").reshape(EXPERTS * BLOCK, LANES)
    (factors,) = call(gates_kernel, [((3, EXPERTS * BLOCK, 3 * n), BF16)], ids, gates)
    return call(combine_kernel, (width // DP, n), back, held(factors)).T


def solution(mesh):
    placed = (
        P(("expert", "tensor"), None),
        P("expert", None),
        P("expert", None),
        P("expert", ("dp", "tensor"), None),
        P("expert", ("dp", "tensor"), None),
        P("expert", ("dp", "tensor"), None),
    )
    return jax.shard_map(
        shards, mesh=mesh, in_specs=placed, out_specs=P(("expert", "tensor"), "dp"), check_vma=False
    )
```

```python
import functools

import jax
import jax.numpy as jnp
from jax import lax
from jax.experimental import pallas as pl
from jax.experimental.pallas import tpu as pltpu
from jax.sharding import PartitionSpec as P

EXPERTS = 16
TOP = 4
CAP = 34
HALF = CAP // 2
SIZE = 4
DP = SIZE * SIZE
LANES = 128
HLANES = 64
BLOCK = 56
SIDE = EXPERTS * HALF
PART = 3 * SIDE
WIDE = 384
MASKS = (3, 1, 2)
F32 = jnp.float32
BF16 = jnp.bfloat16


def quarter(y, x, cut):
    a, b = (y + cut) % SIZE, (x + cut) % SIZE
    return a // 2 * 2 + b // 2, a % 2 * 2 + b % 2


def device(y, x, core):
    return (y % SIZE * SIZE + x % SIZE) * 2 + core


def quarter_groups(back):
    groups = {}
    for core in range(2):
        for y in range(SIZE):
            for x in range(SIZE):
                q, at = quarter(y, x, core ^ back)
                groups.setdefault((core, q), [0] * 4)[at] = device(y, x, core)
    return [groups[key] for key in sorted(groups)]


def across(mask, back):
    pairs = []
    for core in range(2):
        cut = core ^ back
        for y in range(SIZE):
            for x in range(SIZE):
                up = y + 1 if (y + cut) % 2 else y - 1
                right = x + 1 if (x + cut) % 2 else x - 1
                pairs.append((device(y, x, core), device(up if mask & 2 else y, right if mask & 1 else x, core)))
    return pairs


def dot(a, b):
    return jnp.dot(a, b, preferred_element_type=F32)


def dot_t(a, b):
    return lax.dot_general(a, b, (((1,), (1,)), ((), ())), preferred_element_type=F32)


def t_dot(a, b):
    return lax.dot_general(a, b, (((0,), (0,)), ((), ())), preferred_element_type=F32)


def iota(shape, dim):
    return lax.broadcasted_iota(jnp.int32, shape, dim)


def slot_picks(ids):
    n = ids.shape[1]
    named = jnp.zeros((EXPERTS, n), F32)
    for k in range(TOP):
        named += (ids[k : k + 1, :] == iota((EXPERTS, n), 0)).astype(F32)
    earlier = (iota((n, n), 0) < iota((n, n), 1)).astype(BF16)
    slot = jnp.where(named > 0.0, dot(named.astype(BF16), earlier), -1.0)
    rows = EXPERTS * BLOCK

    def expert_of(shape):
        return jnp.floor((iota(shape, 0).astype(F32) + 0.5) * (1.0 / BLOCK))

    spread = (expert_of((rows, EXPERTS)) == iota((rows, EXPERTS), 1).astype(F32)).astype(BF16)
    wide = dot(spread, slot.astype(BF16))
    at = iota((rows, n), 0).astype(F32) - BLOCK * expert_of((rows, n))
    main, half = at < CAP, (at >= CAP) & (at < CAP + HALF)
    return [main & (wide == at), half & (wide == at - CAP), half & (wide == at - HALF)], spread


def dispatch_kernel(ids_ref, tokens_ref, out_ref, columns, sems):
    n = tokens_ref.shape[0]
    core, dp = lax.axis_index("tensor"), lax.axis_index("dp")
    q, at = quarter(dp // SIZE, dp % SIZE, core)
    part = 4 * q + at
    copies = []
    for i, block in enumerate((part, DP + part // 2)):
        lanes = pl.ds(pl.multiple_of(block * LANES, LANES), LANES)
        copies.append(pltpu.make_async_copy(tokens_ref.at[:, lanes], columns.at[i], sems.at[i]))
        copies[i].start()
    picks, _ = slot_picks(ids_ref[:, pl.ds(pl.multiple_of(core * n, n), n)])
    picks = jnp.concatenate([p.astype(BF16) for p in picks], axis=1)
    for copy in copies:
        copy.wait()
    first, rest = columns[0], columns[1].astype(F32)
    low = iota((n, LANES), 1) < HLANES
    turned = pltpu.roll(rest, HLANES, 1)
    odd = part % 2 == 1
    here = jnp.where(odd, turned, rest)
    there = jnp.where(odd, rest, turned)
    rows = jnp.concatenate(
        [first, jnp.where(low, here, 0.0).astype(BF16), jnp.where(low, 0.0, there).astype(BF16)], axis=0
    )
    out_ref[...] = dot(picks, rows).astype(BF16)


def pack_kernel(blocks_ref, out_ref, source, packed):
    source[...] = blocks_ref[...].astype(F32)
    for e in range(EXPERTS):
        for third in range(3):
            packed[third * SIDE + e * HALF : third * SIDE + (e + 1) * HALF, :] = source[
                e * BLOCK + third * HALF : e * BLOCK + (third + 1) * HALF, :
            ]
    value = packed[...].astype(BF16)
    for copy in range(out_ref.shape[0]):
        out_ref[copy] = value


def weights_kernel(gate0, up0, down0, gate1, up1, down1, weights_ref, down_ref):
    hidden, width = gate0.shape
    second = -(-hidden // 16) * 16
    for out_ref, at, pair in ((weights_ref, 0, (gate0, gate1)), (weights_ref, WIDE, (up0, up1)), (down_ref, 0, (down0, down1))):
        for start, ref, end in ((0, pair[0], second), (second, pair[1], WIDE)):
            out_ref[at + start : at + start + hidden, :] = ref[...]
            out_ref[at + start + hidden : at + end, :] = jnp.zeros((end - start - hidden, width), BF16)


def place_of(back):
    cut, dp = lax.axis_index("tensor") ^ back, lax.axis_index("dp")
    return cut, quarter(dp // SIZE, dp % SIZE, cut)[0]


def products(mask, x_ref, weights_ref):
    _, q = place_of(0)
    q = q ^ mask
    low = iota((SIDE, LANES), 1) < HLANES
    main = jnp.concatenate([x_ref[at, : 2 * SIDE, :] for at in range(4)], axis=1)
    halves = []
    for pair in range(2):
        even = x_ref[2 * pair, 2 * SIDE :, :].astype(F32)
        odd = x_ref[2 * pair + 1, 2 * SIDE :, :].astype(F32)
        upper = jnp.where(low, even, pltpu.roll(odd, HLANES, 1)).astype(BF16)
        lower = jnp.where(low, pltpu.roll(even, HLANES, 1), odd).astype(BF16)
        halves.append(jnp.concatenate([upper, lower], axis=0))
    rest = jnp.concatenate(halves, axis=1)
    main_lanes = pl.ds(pl.multiple_of(q * 4 * LANES, LANES), 4 * LANES)
    rest_lanes = pl.ds(pl.multiple_of((DP + q * 2) * LANES, LANES), 2 * LANES)
    return dot_t(main, weights_ref[:, main_lanes]) + dot_t(rest, weights_ref[:, rest_lanes])


def down_products(mask, hidden, down_ref, out_ref):
    cut, q = place_of(1)
    to = q ^ mask
    lane = iota((SIDE, LANES), 1)
    for at in range(4):
        dp = (to // 2 * 2 + at // 2 - cut) % SIZE * SIZE + (to % 2 * 2 + at % 2 - cut) % SIZE
        odd = dp % 2
        main = (3 * dp + odd) // 2
        blocks = [pl.ds(pl.multiple_of(i * LANES, LANES), LANES) for i in (main, main + 1 - 2 * odd)]
        y = dot(hidden, jnp.concatenate([down_ref[:, lanes] for lanes in blocks], axis=1))
        out_ref[at, : 2 * SIDE, :] = y[:, :LANES].astype(BF16)
        upper, lower = y[:SIDE, LANES:], y[SIDE:, LANES:]
        stays = jnp.where(odd == 1, lower, upper)
        turned = pltpu.roll(jnp.where(odd == 1, upper, lower), HLANES, 1)
        out_ref[at, 2 * SIDE :, :] = jnp.where(lane ^ (odd * HLANES) < HLANES, stays, turned).astype(BF16)


def first_kernel(mask, x_ref, weights_ref, total_ref):
    total_ref[...] = products(mask, x_ref, weights_ref)


def next_kernel(mask, x_ref, weights_ref, sofar_ref, total_ref):
    total_ref[...] = sofar_ref[...] + products(mask, x_ref, weights_ref)


def last_kernel(mask, x_ref, weights_ref, sofar_ref, down_ref, hidden_ref, *out_refs):
    total = sofar_ref[...] + products(mask, x_ref, weights_ref)
    g, u = total[:, :WIDE], total[:, WIDE:]
    hidden = (g / (1.0 + jnp.exp(-g)) * u).astype(BF16)
    hidden_ref[...] = hidden
    for to, out_ref in zip(MASKS, out_refs):
        down_products(to, hidden, down_ref, out_ref)


def down_kernel(mask, hidden_ref, down_ref, out_ref):
    down_products(mask, hidden_ref[...], down_ref, out_ref)


def add_kernel(a, b, out_ref):
    out_ref[...] = (a[...].astype(F32) + b[...].astype(F32)).astype(out_ref.dtype)


def add_blocks_kernel(parts_ref, out_ref, packed, blocks):
    total = parts_ref[0].astype(F32)
    for i in range(1, parts_ref.shape[0]):
        total += parts_ref[i].astype(F32)
    packed[...] = total
    for e in range(EXPERTS):
        for third in range(3):
            blocks[e * BLOCK + third * HALF : e * BLOCK + (third + 1) * HALF, :] = packed[
                third * SIDE + e * HALF : third * SIDE + (e + 1) * HALF, :
            ]
        blocks[e * BLOCK + 3 * HALF : (e + 1) * BLOCK, :] = jnp.zeros((BLOCK - 3 * HALF, LANES), F32)
    out_ref[...] = blocks[...].astype(BF16)


def gates_kernel(ids_ref, gates_ref, out_ref):
    n = out_ref.shape[2] // 3
    own = pl.ds(pl.multiple_of(lax.axis_index("tensor") * n, n), n)
    ids, given = ids_ref[:, own], gates_ref[:, own]
    picks, spread = slot_picks(ids)
    picks = jnp.concatenate(picks, axis=1)
    gates = jnp.zeros((EXPERTS, n), F32)
    for k in range(TOP):
        gates += jnp.where(ids[k : k + 1, :] == iota((EXPERTS, n), 0), given[k : k + 1, :], 0.0)
    for i in range(3):
        piece = gates.astype(BF16)
        gates = gates - piece.astype(F32)
        weight = dot(spread, piece)
        weight = jnp.concatenate([weight, weight, weight], axis=1)
        out_ref[i] = jnp.where(picks, weight, 0.0).astype(BF16)


def combine_kernel(blocks_ref, gates_ref, out_ref):
    n = out_ref.shape[1]
    blocks = blocks_ref[...]
    total = t_dot(blocks, gates_ref[0]) + t_dot(blocks, gates_ref[1]) + t_dot(blocks, gates_ref[2])
    first = total[:, :n]
    rest = total[:HLANES, n : 2 * n] + total[HLANES:, 2 * n :]
    odd = lax.axis_index("dp") % 2 == 1
    out_ref[:HLANES, :] = jnp.where(odd, rest, first[:HLANES]).astype(BF16)
    out_ref[HLANES:LANES, :] = jnp.where(odd, first[:HLANES], first[HLANES:]).astype(BF16)
    out_ref[LANES:, :] = jnp.where(odd, first[HLANES:], rest).astype(BF16)


def call(kernel, shape, *args, scratch=(), limit=16, specs=None):
    out = jax.ShapeDtypeStruct(shape, BF16) if isinstance(shape, tuple) else [pltpu.VMEM(s, d) for s, d in shape]
    places = {} if specs is None else {"in_specs": [pl.BlockSpec(memory_space=space) for space in specs]}
    return pl.pallas_call(
        kernel,
        out_shape=out,
        **places,
        scratch_shapes=scratch,
        compiler_params=pltpu.CompilerParams(vmem_limit_bytes=limit * 1024 * 1024),
    )(*args)


def held(value):
    return pltpu.with_memory_space_constraint(value, pltpu.VMEM)


def swap(value):
    return lax.ppermute(value, "tensor", [(0, 1), (1, 0)])


def exchange(value, axis, groups=None):
    return lax.all_to_all(value, axis, split_axis=0, concat_axis=0, tiled=True, axis_index_groups=groups)


def shards(tokens, expert_ids, gate_values, w_gate, w_up, w_down):
    n, width = tokens.shape
    plane = ("dp", "tensor")
    ids, gates = expert_ids.T, gate_values.T
    own = [w_gate[0], w_up[0], w_down[0]]
    weights, down = call(
        weights_kernel, [((2 * WIDE, width), BF16), ((WIDE, width), BF16)], *own, *map(swap, own), limit=24
    )
    weights, down = held(weights), held(down)
    part_scratch = pltpu.VMEM((PART, LANES), F32)
    block_scratch = pltpu.VMEM((EXPERTS * BLOCK, LANES), F32)

    sent = call(
        dispatch_kernel,
        (EXPERTS * BLOCK, LANES),
        *(ids, tokens),
        scratch=[pltpu.VMEM((2, n, LANES), BF16), pltpu.SemaphoreType.DMA((2,))],
        specs=(pltpu.VMEM, pltpu.HBM),
    )
    arrived = exchange(sent.reshape(EXPERTS, BLOCK, LANES), "expert").reshape(EXPERTS * BLOCK, LANES)
    rows = call(pack_kernel, (4, PART, LANES), arrived, scratch=[block_scratch, part_scratch])
    rows = exchange(rows, plane, quarter_groups(0))
    others = [lax.ppermute(rows, plane, across(mask, 0)) for mask in MASKS]
    total_shape, out_shape = ((2 * SIDE, 2 * WIDE), F32), ((4, PART, LANES), BF16)
    (total,) = call(functools.partial(first_kernel, 0), [total_shape], rows, weights, limit=32)
    for mask, other in zip(MASKS[:2], others[:2]):
        (total,) = call(functools.partial(next_kernel, mask), [total_shape], other, weights, held(total), limit=32)
    hidden, *outs = call(
        functools.partial(last_kernel, MASKS[2]),
        [((2 * SIDE, WIDE), BF16)] + [out_shape] * 3,
        *(others[2], weights, held(total), down),
        limit=32,
    )
    (partial,) = call(functools.partial(down_kernel, 0), [out_shape], held(hidden), down, limit=32)
    others = [lax.ppermute(out, plane, across(mask, 1)) for mask, out in zip(MASKS, outs)]
    for other, kind in zip(others, (F32, F32, BF16)):
        (partial,) = call(add_kernel, [((4, PART, LANES), kind)], held(partial), other, limit=24)
    partial = exchange(partial, plane, quarter_groups(1))
    summed = call(add_blocks_kernel, (EXPERTS * BLOCK, LANES), partial, scratch=[part_scratch, block_scratch])
    back = exchange(summed.reshape(EXPERTS, BLOCK, LANES), "expert").reshape(EXPERTS * BLOCK, LANES)
    (factors,) = call(gates_kernel, [((3, EXPERTS * BLOCK, 3 * n), BF16)], ids, gates)
    return call(combine_kernel, (width // DP, n), back, held(factors)).T


def solution(mesh):
    placed = (
        P(("expert", "tensor"), None),
        P("expert", None),
        P("expert", None),
        P("expert", ("dp", "tensor"), None),
        P("expert", ("dp", "tensor"), None),
        P("expert", ("dp", "tensor"), None),
    )
    return jax.shard_map(
        shards, mesh=mesh, in_specs=placed, out_specs=P(("expert", "tensor"), "dp"), check_vma=False
    )
```

```python
import functools

import jax
import jax.numpy as jnp
from jax import lax
from jax.experimental import pallas as pl
from jax.experimental.pallas import tpu as pltpu
from jax.sharding import PartitionSpec as P

EXPERTS = 16
TOP = 4
CAP = 34
HALF = CAP // 2
SIZE = 4
DP = SIZE * SIZE
LANES = 128
HLANES = 64
BLOCK = 56
SIDE = EXPERTS * HALF
PART = 3 * SIDE
WIDE = 384
MASKS = (3, 1, 2)
F32 = jnp.float32
BF16 = jnp.bfloat16


def quarter(y, x, cut):
    a, b = (y + cut) % SIZE, (x + cut) % SIZE
    return a // 2 * 2 + b // 2, a % 2 * 2 + b % 2


def device(y, x, core):
    return (y % SIZE * SIZE + x % SIZE) * 2 + core


def quarter_groups(back):
    groups = {}
    for core in range(2):
        for y in range(SIZE):
            for x in range(SIZE):
                q, at = quarter(y, x, core ^ back)
                groups.setdefault((core, q), [0] * 4)[at] = device(y, x, core)
    return [groups[key] for key in sorted(groups)]


def across(mask, back):
    pairs = []
    for core in range(2):
        cut = core ^ back
        for y in range(SIZE):
            for x in range(SIZE):
                up = y + 1 if (y + cut) % 2 else y - 1
                right = x + 1 if (x + cut) % 2 else x - 1
                pairs.append((device(y, x, core), device(up if mask & 2 else y, right if mask & 1 else x, core)))
    return pairs


def dot(a, b):
    return jnp.dot(a, b, preferred_element_type=F32)


def dot_t(a, b):
    return lax.dot_general(a, b, (((1,), (1,)), ((), ())), preferred_element_type=F32)


def t_dot(a, b):
    return lax.dot_general(a, b, (((0,), (0,)), ((), ())), preferred_element_type=F32)


def iota(shape, dim):
    return lax.broadcasted_iota(jnp.int32, shape, dim)


def slot_picks(ids):
    n = ids.shape[1]
    named = jnp.zeros((EXPERTS, n), F32)
    for k in range(TOP):
        named += (ids[k : k + 1, :] == iota((EXPERTS, n), 0)).astype(F32)
    earlier = (iota((n, n), 0) < iota((n, n), 1)).astype(BF16)
    slot = jnp.where(named > 0.0, dot(named.astype(BF16), earlier), -1.0)
    rows = EXPERTS * BLOCK

    def expert_of(shape):
        return jnp.floor((iota(shape, 0).astype(F32) + 0.5) * (1.0 / BLOCK))

    spread = (expert_of((rows, EXPERTS)) == iota((rows, EXPERTS), 1).astype(F32)).astype(BF16)
    wide = dot(spread, slot.astype(BF16))
    at = iota((rows, n), 0).astype(F32) - BLOCK * expert_of((rows, n))
    main, half = at < CAP, (at >= CAP) & (at < CAP + HALF)
    return [main & (wide == at), half & (wide == at - CAP), half & (wide == at - HALF)], spread


def dispatch_kernel(ids_ref, tokens_ref, out_ref, columns, sems):
    n = tokens_ref.shape[0]
    core, dp = lax.axis_index("tensor"), lax.axis_index("dp")
    q, at = quarter(dp // SIZE, dp % SIZE, core)
    part = 4 * q + at
    copies = []
    for i, block in enumerate((part, DP + part // 2)):
        lanes = pl.ds(pl.multiple_of(block * LANES, LANES), LANES)
        copies.append(pltpu.make_async_copy(tokens_ref.at[:, lanes], columns.at[i], sems.at[i]))
        copies[i].start()
    picks, _ = slot_picks(ids_ref[:, pl.ds(pl.multiple_of(core * n, n), n)])
    picks = jnp.concatenate([p.astype(BF16) for p in picks], axis=1)
    for copy in copies:
        copy.wait()
    first, rest = columns[0], columns[1].astype(F32)
    low = iota((n, LANES), 1) < HLANES
    turned = pltpu.roll(rest, HLANES, 1)
    odd = part % 2 == 1
    here = jnp.where(odd, turned, rest)
    there = jnp.where(odd, rest, turned)
    rows = jnp.concatenate(
        [first, jnp.where(low, here, 0.0).astype(BF16), jnp.where(low, 0.0, there).astype(BF16)], axis=0
    )
    out_ref[...] = dot(picks, rows).astype(BF16)


def pack_kernel(blocks_ref, out_ref, source, packed):
    source[...] = blocks_ref[...].astype(F32)
    for e in range(EXPERTS):
        for third in range(3):
            packed[third * SIDE + e * HALF : third * SIDE + (e + 1) * HALF, :] = source[
                e * BLOCK + third * HALF : e * BLOCK + (third + 1) * HALF, :
            ]
    value = packed[...].astype(BF16)
    for copy in range(out_ref.shape[0]):
        out_ref[copy] = value


def weights_kernel(gate0, up0, down0, gate1, up1, down1, weights_ref, down_ref):
    hidden, width = gate0.shape
    second = -(-hidden // 16) * 16
    for out_ref, at, pair in ((weights_ref, 0, (gate0, gate1)), (weights_ref, WIDE, (up0, up1)), (down_ref, 0, (down0, down1))):
        for start, ref, end in ((0, pair[0], second), (second, pair[1], WIDE)):
            out_ref[at + start : at + start + hidden, :] = ref[...]
            out_ref[at + start + hidden : at + end, :] = jnp.zeros((end - start - hidden, width), BF16)


def place_of(back):
    cut, dp = lax.axis_index("tensor") ^ back, lax.axis_index("dp")
    return cut, quarter(dp // SIZE, dp % SIZE, cut)[0]


def products(mask, x_ref, weights_ref):
    _, q = place_of(0)
    q = q ^ mask
    low = iota((SIDE, LANES), 1) < HLANES
    main = jnp.concatenate([x_ref[at, : 2 * SIDE, :] for at in range(4)], axis=1)
    halves = []
    for pair in range(2):
        even = x_ref[2 * pair, 2 * SIDE :, :].astype(F32)
        odd = x_ref[2 * pair + 1, 2 * SIDE :, :].astype(F32)
        upper = jnp.where(low, even, pltpu.roll(odd, HLANES, 1)).astype(BF16)
        lower = jnp.where(low, pltpu.roll(even, HLANES, 1), odd).astype(BF16)
        halves.append(jnp.concatenate([upper, lower], axis=0))
    rest = jnp.concatenate(halves, axis=1)
    main_lanes = pl.ds(pl.multiple_of(q * 4 * LANES, LANES), 4 * LANES)
    rest_lanes = pl.ds(pl.multiple_of((DP + q * 2) * LANES, LANES), 2 * LANES)
    return dot_t(main, weights_ref[:, main_lanes]) + dot_t(rest, weights_ref[:, rest_lanes])


def down_products(mask, hidden, down_ref, out_ref):
    cut, q = place_of(1)
    to = q ^ mask
    lane = iota((SIDE, LANES), 1)
    for at in range(4):
        dp = (to // 2 * 2 + at // 2 - cut) % SIZE * SIZE + (to % 2 * 2 + at % 2 - cut) % SIZE
        odd = dp % 2
        main = (3 * dp + odd) // 2
        blocks = [pl.ds(pl.multiple_of(i * LANES, LANES), LANES) for i in (main, main + 1 - 2 * odd)]
        y = dot(hidden, jnp.concatenate([down_ref[:, lanes] for lanes in blocks], axis=1))
        out_ref[at, : 2 * SIDE, :] = y[:, :LANES].astype(BF16)
        upper, lower = y[:SIDE, LANES:], y[SIDE:, LANES:]
        stays = jnp.where(odd == 1, lower, upper)
        turned = pltpu.roll(jnp.where(odd == 1, upper, lower), HLANES, 1)
        out_ref[at, 2 * SIDE :, :] = jnp.where(lane ^ (odd * HLANES) < HLANES, stays, turned).astype(BF16)


def first_kernel(mask, x_ref, weights_ref, total_ref):
    total_ref[...] = products(mask, x_ref, weights_ref)


def next_kernel(mask, x_ref, weights_ref, sofar_ref, total_ref):
    total_ref[...] = sofar_ref[...] + products(mask, x_ref, weights_ref)


def last_kernel(mask, x_ref, weights_ref, sofar_ref, down_ref, hidden_ref, *out_refs):
    total = sofar_ref[...] + products(mask, x_ref, weights_ref)
    g, u = total[:, :WIDE], total[:, WIDE:]
    hidden = (g / (1.0 + jnp.exp(-g)) * u).astype(BF16)
    hidden_ref[...] = hidden
    for to, out_ref in zip(MASKS, out_refs):
        down_products(to, hidden, down_ref, out_ref)


def down_kernel(mask, hidden_ref, down_ref, out_ref):
    down_products(mask, hidden_ref[...], down_ref, out_ref)


def add_kernel(a, b, out_ref):
    out_ref[...] = (a[...].astype(F32) + b[...].astype(F32)).astype(out_ref.dtype)


def add_blocks_kernel(parts_ref, out_ref, packed, blocks):
    total = parts_ref[0].astype(F32)
    for i in range(1, parts_ref.shape[0]):
        total += parts_ref[i].astype(F32)
    packed[...] = total
    for e in range(EXPERTS):
        for third in range(3):
            blocks[e * BLOCK + third * HALF : e * BLOCK + (third + 1) * HALF, :] = packed[
                third * SIDE + e * HALF : third * SIDE + (e + 1) * HALF, :
            ]
        blocks[e * BLOCK + 3 * HALF : (e + 1) * BLOCK, :] = jnp.zeros((BLOCK - 3 * HALF, LANES), F32)
    out_ref[...] = blocks[...].astype(BF16)


def gates_kernel(ids_ref, gates_ref, out_ref):
    n = out_ref.shape[2] // 3
    own = pl.ds(pl.multiple_of(lax.axis_index("tensor") * n, n), n)
    ids, given = ids_ref[:, own], gates_ref[:, own]
    picks, spread = slot_picks(ids)
    picks = jnp.concatenate(picks, axis=1)
    gates = jnp.zeros((EXPERTS, n), F32)
    for k in range(TOP):
        gates += jnp.where(ids[k : k + 1, :] == iota((EXPERTS, n), 0), given[k : k + 1, :], 0.0)
    for i in range(3):
        piece = gates.astype(BF16)
        gates = gates - piece.astype(F32)
        weight = dot(spread, piece)
        weight = jnp.concatenate([weight, weight, weight], axis=1)
        out_ref[i] = jnp.where(picks, weight, 0.0).astype(BF16)


def combine_kernel(blocks_ref, gates_ref, out_ref):
    n = out_ref.shape[1]
    blocks = blocks_ref[...]
    total = t_dot(blocks, gates_ref[0]) + t_dot(blocks, gates_ref[1]) + t_dot(blocks, gates_ref[2])
    first = total[:, :n]
    rest = total[:HLANES, n : 2 * n] + total[HLANES:, 2 * n :]
    odd = lax.axis_index("dp") % 2 == 1
    out_ref[:HLANES, :] = jnp.where(odd, rest, first[:HLANES]).astype(BF16)
    out_ref[HLANES:LANES, :] = jnp.where(odd, first[:HLANES], first[HLANES:]).astype(BF16)
    out_ref[LANES:, :] = jnp.where(odd, first[HLANES:], rest).astype(BF16)


def call(kernel, shape, *args, scratch=(), limit=16, specs=None):
    out = jax.ShapeDtypeStruct(shape, BF16) if isinstance(shape, tuple) else [pltpu.VMEM(s, d) for s, d in shape]
    places = {} if specs is None else {"in_specs": [pl.BlockSpec(memory_space=space) for space in specs]}
    return pl.pallas_call(
        kernel,
        out_shape=out,
        **places,
        scratch_shapes=scratch,
        compiler_params=pltpu.CompilerParams(vmem_limit_bytes=limit * 1024 * 1024),
    )(*args)


def held(value):
    return pltpu.with_memory_space_constraint(value, pltpu.VMEM)


def swap(value):
    return lax.ppermute(value, "tensor", [(0, 1), (1, 0)])


def exchange(value, axis, groups=None):
    return lax.all_to_all(value, axis, split_axis=0, concat_axis=0, tiled=True, axis_index_groups=groups)


def shards(tokens, expert_ids, gate_values, w_gate, w_up, w_down):
    n, width = tokens.shape
    plane = ("dp", "tensor")
    ids, gates = expert_ids.T, gate_values.T
    own = [w_gate[0], w_up[0], w_down[0]]
    weights, down = call(
        weights_kernel, [((2 * WIDE, width), BF16), ((WIDE, width), BF16)], *own, *map(swap, own), limit=24
    )
    weights, down = held(weights), held(down)
    part_scratch = pltpu.VMEM((PART, LANES), F32)
    block_scratch = pltpu.VMEM((EXPERTS * BLOCK, LANES), F32)

    sent = call(
        dispatch_kernel,
        (EXPERTS * BLOCK, LANES),
        *(ids, pltpu.with_memory_space_constraint(tokens, pltpu.HBM)),
        scratch=[pltpu.VMEM((2, n, LANES), BF16), pltpu.SemaphoreType.DMA((2,))],
        specs=(pltpu.VMEM, pltpu.HBM),
    )
    arrived = exchange(sent.reshape(EXPERTS, BLOCK, LANES), "expert").reshape(EXPERTS * BLOCK, LANES)
    rows = call(pack_kernel, (4, PART, LANES), arrived, scratch=[block_scratch, part_scratch])
    rows = exchange(rows, plane, quarter_groups(0))
    others = [lax.ppermute(rows, plane, across(mask, 0)) for mask in MASKS]
    total_shape, out_shape = ((2 * SIDE, 2 * WIDE), F32), ((4, PART, LANES), BF16)
    (total,) = call(functools.partial(first_kernel, 0), [total_shape], rows, weights, limit=32)
    for mask, other in zip(MASKS[:2], others[:2]):
        (total,) = call(functools.partial(next_kernel, mask), [total_shape], other, weights, held(total), limit=32)
    hidden, *outs = call(
        functools.partial(last_kernel, MASKS[2]),
        [((2 * SIDE, WIDE), BF16)] + [out_shape] * 3,
        *(others[2], weights, held(total), down),
        limit=32,
    )
    (partial,) = call(functools.partial(down_kernel, 0), [out_shape], held(hidden), down, limit=32)
    others = [lax.ppermute(out, plane, across(mask, 1)) for mask, out in zip(MASKS, outs)]
    for other, kind in zip(others, (F32, F32, BF16)):
        (partial,) = call(add_kernel, [((4, PART, LANES), kind)], held(partial), other, limit=24)
    partial = exchange(partial, plane, quarter_groups(1))
    summed = call(add_blocks_kernel, (EXPERTS * BLOCK, LANES), partial, scratch=[part_scratch, block_scratch])
    back = exchange(summed.reshape(EXPERTS, BLOCK, LANES), "expert").reshape(EXPERTS * BLOCK, LANES)
    (factors,) = call(gates_kernel, [((3, EXPERTS * BLOCK, 3 * n), BF16)], ids, gates)
    return call(combine_kernel, (width // DP, n), back, held(factors)).T


def solution(mesh):
    placed = (
        P(("expert", "tensor"), None),
        P("expert", None),
        P("expert", None),
        P("expert", ("dp", "tensor"), None),
        P("expert", ("dp", "tensor"), None),
        P("expert", ("dp", "tensor"), None),
    )
    return jax.shard_map(
        shards, mesh=mesh, in_specs=placed, out_specs=P(("expert", "tensor"), "dp"), check_vma=False
    )
```

```python
import functools

import jax
import jax.numpy as jnp
from jax import lax
from jax.experimental import pallas as pl
from jax.experimental.pallas import tpu as pltpu
from jax.sharding import PartitionSpec as P

EXPERTS = 16
TOP = 4
CAP = 34
HALF = CAP // 2
SIZE = 4
DP = SIZE * SIZE
LANES = 128
HLANES = 64
BLOCK = 56
SIDE = EXPERTS * HALF
PART = 3 * SIDE
WIDE = 384
MASKS = (3, 2, 1)
F32 = jnp.float32
BF16 = jnp.bfloat16


def quarter(y, x, cut):
    a, b = (y + cut) % SIZE, (x + cut) % SIZE
    return a // 2 * 2 + b // 2, a % 2 * 2 + b % 2


def device(y, x, core):
    return (y % SIZE * SIZE + x % SIZE) * 2 + core


def quarter_groups(back):
    groups = {}
    for core in range(2):
        for y in range(SIZE):
            for x in range(SIZE):
                q, at = quarter(y, x, core ^ back)
                groups.setdefault((core, q), [0] * 4)[at] = device(y, x, core)
    return [groups[key] for key in sorted(groups)]


def across(mask, back):
    pairs = []
    for core in range(2):
        cut = core ^ back
        for y in range(SIZE):
            for x in range(SIZE):
                up = y + 1 if (y + cut) % 2 else y - 1
                right = x + 1 if (x + cut) % 2 else x - 1
                pairs.append((device(y, x, core), device(up if mask & 2 else y, right if mask & 1 else x, core)))
    return pairs


def dot(a, b):
    return jnp.dot(a, b, preferred_element_type=F32)


def dot_t(a, b):
    return lax.dot_general(a, b, (((1,), (1,)), ((), ())), preferred_element_type=F32)


def t_dot(a, b):
    return lax.dot_general(a, b, (((0,), (0,)), ((), ())), preferred_element_type=F32)


def iota(shape, dim):
    return lax.broadcasted_iota(jnp.int32, shape, dim)


def slot_picks(ids):
    n = ids.shape[1]
    named = jnp.zeros((EXPERTS, n), F32)
    for k in range(TOP):
        named += (ids[k : k + 1, :] == iota((EXPERTS, n), 0)).astype(F32)
    earlier = (iota((n, n), 0) < iota((n, n), 1)).astype(BF16)
    slot = jnp.where(named > 0.0, dot(named.astype(BF16), earlier), -1.0)
    rows = EXPERTS * BLOCK

    def expert_of(shape):
        return jnp.floor((iota(shape, 0).astype(F32) + 0.5) * (1.0 / BLOCK))

    spread = (expert_of((rows, EXPERTS)) == iota((rows, EXPERTS), 1).astype(F32)).astype(BF16)
    wide = dot(spread, slot.astype(BF16))
    at = iota((rows, n), 0).astype(F32) - BLOCK * expert_of((rows, n))
    main, half = at < CAP, (at >= CAP) & (at < CAP + HALF)
    return [main & (wide == at), half & (wide == at - CAP), half & (wide == at - HALF)], spread


def dispatch_kernel(ids_ref, tokens_ref, out_ref, columns, sems):
    n = tokens_ref.shape[0]
    core, dp = lax.axis_index("tensor"), lax.axis_index("dp")
    q, at = quarter(dp // SIZE, dp % SIZE, core)
    part = 4 * q + at
    copies = []
    for i, block in enumerate((part, DP + part // 2)):
        lanes = pl.ds(pl.multiple_of(block * LANES, LANES), LANES)
        copies.append(pltpu.make_async_copy(tokens_ref.at[:, lanes], columns.at[i], sems.at[i]))
        copies[i].start()
    picks, _ = slot_picks(ids_ref[:, pl.ds(pl.multiple_of(core * n, n), n)])
    picks = jnp.concatenate([p.astype(BF16) for p in picks], axis=1)
    for copy in copies:
        copy.wait()
    first, rest = columns[0], columns[1].astype(F32)
    low = iota((n, LANES), 1) < HLANES
    turned = pltpu.roll(rest, HLANES, 1)
    odd = part % 2 == 1
    here = jnp.where(odd, turned, rest)
    there = jnp.where(odd, rest, turned)
    rows = jnp.concatenate(
        [first, jnp.where(low, here, 0.0).astype(BF16), jnp.where(low, 0.0, there).astype(BF16)], axis=0
    )
    out_ref[...] = dot(picks, rows).astype(BF16)


def pack_kernel(blocks_ref, out_ref, source, packed):
    source[...] = blocks_ref[...].astype(F32)
    for e in range(EXPERTS):
        for third in range(3):
            packed[third * SIDE + e * HALF : third * SIDE + (e + 1) * HALF, :] = source[
                e * BLOCK + third * HALF : e * BLOCK + (third + 1) * HALF, :
            ]
    value = packed[...].astype(BF16)
    for copy in range(out_ref.shape[0]):
        out_ref[copy] = value


def weights_kernel(gate0, up0, down0, gate1, up1, down1, weights_ref, down_ref):
    hidden, width = gate0.shape
    second = -(-hidden // 16) * 16
    for out_ref, at, pair in ((weights_ref, 0, (gate0, gate1)), (weights_ref, WIDE, (up0, up1)), (down_ref, 0, (down0, down1))):
        for start, ref, end in ((0, pair[0], second), (second, pair[1], WIDE)):
            out_ref[at + start : at + start + hidden, :] = ref[...]
            out_ref[at + start + hidden : at + end, :] = jnp.zeros((end - start - hidden, width), BF16)


def place_of(back):
    cut, dp = lax.axis_index("tensor") ^ back, lax.axis_index("dp")
    return cut, quarter(dp // SIZE, dp % SIZE, cut)[0]


def products(mask, x_ref, weights_ref):
    _, q = place_of(0)
    q = q ^ mask
    low = iota((SIDE, LANES), 1) < HLANES
    main = jnp.concatenate([x_ref[at, : 2 * SIDE, :] for at in range(4)], axis=1)
    halves = []
    for pair in range(2):
        even = x_ref[2 * pair, 2 * SIDE :, :].astype(F32)
        odd = x_ref[2 * pair + 1, 2 * SIDE :, :].astype(F32)
        upper = jnp.where(low, even, pltpu.roll(odd, HLANES, 1)).astype(BF16)
        lower = jnp.where(low, pltpu.roll(even, HLANES, 1), odd).astype(BF16)
        halves.append(jnp.concatenate([upper, lower], axis=0))
    rest = jnp.concatenate(halves, axis=1)
    main_lanes = pl.ds(pl.multiple_of(q * 4 * LANES, LANES), 4 * LANES)
    rest_lanes = pl.ds(pl.multiple_of((DP + q * 2) * LANES, LANES), 2 * LANES)
    return dot_t(main, weights_ref[:, main_lanes]) + dot_t(rest, weights_ref[:, rest_lanes])


def down_products(mask, hidden, down_ref, out_ref):
    cut, q = place_of(1)
    to = q ^ mask
    lane = iota((SIDE, LANES), 1)
    for at in range(4):
        dp = (to // 2 * 2 + at // 2 - cut) % SIZE * SIZE + (to % 2 * 2 + at % 2 - cut) % SIZE
        odd = dp % 2
        main = (3 * dp + odd) // 2
        blocks = [pl.ds(pl.multiple_of(i * LANES, LANES), LANES) for i in (main, main + 1 - 2 * odd)]
        y = dot(hidden, jnp.concatenate([down_ref[:, lanes] for lanes in blocks], axis=1))
        out_ref[at, : 2 * SIDE, :] = y[:, :LANES].astype(BF16)
        upper, lower = y[:SIDE, LANES:], y[SIDE:, LANES:]
        stays = jnp.where(odd == 1, lower, upper)
        turned = pltpu.roll(jnp.where(odd == 1, upper, lower), HLANES, 1)
        out_ref[at, 2 * SIDE :, :] = jnp.where(lane ^ (odd * HLANES) < HLANES, stays, turned).astype(BF16)


def first_kernel(mask, x_ref, weights_ref, total_ref):
    total_ref[...] = products(mask, x_ref, weights_ref)


def next_kernel(mask, x_ref, weights_ref, sofar_ref, total_ref):
    total_ref[...] = sofar_ref[...] + products(mask, x_ref, weights_ref)


def last_kernel(mask, x_ref, weights_ref, sofar_ref, down_ref, hidden_ref, *out_refs):
    total = sofar_ref[...] + products(mask, x_ref, weights_ref)
    g, u = total[:, :WIDE], total[:, WIDE:]
    hidden = (g / (1.0 + jnp.exp(-g)) * u).astype(BF16)
    hidden_ref[...] = hidden
    for to, out_ref in zip(MASKS, out_refs):
        down_products(to, hidden, down_ref, out_ref)


def down_kernel(mask, hidden_ref, down_ref, out_ref):
    down_products(mask, hidden_ref[...], down_ref, out_ref)


def add_kernel(a, b, out_ref):
    out_ref[...] = (a[...].astype(F32) + b[...].astype(F32)).astype(out_ref.dtype)


def add_blocks_kernel(parts_ref, out_ref, packed, blocks):
    total = parts_ref[0].astype(F32)
    for i in range(1, parts_ref.shape[0]):
        total += parts_ref[i].astype(F32)
    packed[...] = total
    for e in range(EXPERTS):
        for third in range(3):
            blocks[e * BLOCK + third * HALF : e * BLOCK + (third + 1) * HALF, :] = packed[
                third * SIDE + e * HALF : third * SIDE + (e + 1) * HALF, :
            ]
        blocks[e * BLOCK + 3 * HALF : (e + 1) * BLOCK, :] = jnp.zeros((BLOCK - 3 * HALF, LANES), F32)
    out_ref[...] = blocks[...].astype(BF16)


def gates_kernel(ids_ref, gates_ref, out_ref):
    n = out_ref.shape[2] // 3
    own = pl.ds(pl.multiple_of(lax.axis_index("tensor") * n, n), n)
    ids, given = ids_ref[:, own], gates_ref[:, own]
    picks, spread = slot_picks(ids)
    picks = jnp.concatenate(picks, axis=1)
    gates = jnp.zeros((EXPERTS, n), F32)
    for k in range(TOP):
        gates += jnp.where(ids[k : k + 1, :] == iota((EXPERTS, n), 0), given[k : k + 1, :], 0.0)
    for i in range(3):
        piece = gates.astype(BF16)
        gates = gates - piece.astype(F32)
        weight = dot(spread, piece)
        weight = jnp.concatenate([weight, weight, weight], axis=1)
        out_ref[i] = jnp.where(picks, weight, 0.0).astype(BF16)


def combine_kernel(blocks_ref, gates_ref, out_ref):
    n = out_ref.shape[1]
    blocks = blocks_ref[...]
    total = t_dot(blocks, gates_ref[0]) + t_dot(blocks, gates_ref[1]) + t_dot(blocks, gates_ref[2])
    first = total[:, :n]
    rest = total[:HLANES, n : 2 * n] + total[HLANES:, 2 * n :]
    odd = lax.axis_index("dp") % 2 == 1
    out_ref[:HLANES, :] = jnp.where(odd, rest, first[:HLANES]).astype(BF16)
    out_ref[HLANES:LANES, :] = jnp.where(odd, first[:HLANES], first[HLANES:]).astype(BF16)
    out_ref[LANES:, :] = jnp.where(odd, first[HLANES:], rest).astype(BF16)


def call(kernel, shape, *args, scratch=(), limit=16, specs=None):
    out = jax.ShapeDtypeStruct(shape, BF16) if isinstance(shape, tuple) else [pltpu.VMEM(s, d) for s, d in shape]
    places = {} if specs is None else {"in_specs": [pl.BlockSpec(memory_space=space) for space in specs]}
    return pl.pallas_call(
        kernel,
        out_shape=out,
        **places,
        scratch_shapes=scratch,
        compiler_params=pltpu.CompilerParams(vmem_limit_bytes=limit * 1024 * 1024),
    )(*args)


def held(value):
    return pltpu.with_memory_space_constraint(value, pltpu.VMEM)


def swap(value):
    return lax.ppermute(value, "tensor", [(0, 1), (1, 0)])


def exchange(value, axis, groups=None):
    return lax.all_to_all(value, axis, split_axis=0, concat_axis=0, tiled=True, axis_index_groups=groups)


def shards(tokens, expert_ids, gate_values, w_gate, w_up, w_down):
    n, width = tokens.shape
    plane = ("dp", "tensor")
    ids, gates = expert_ids.T, gate_values.T
    own = [w_gate[0], w_up[0], w_down[0]]
    weights, down = call(
        weights_kernel, [((2 * WIDE, width), BF16), ((WIDE, width), BF16)], *own, *map(swap, own), limit=24
    )
    weights, down = held(weights), held(down)
    part_scratch = pltpu.VMEM((PART, LANES), F32)
    block_scratch = pltpu.VMEM((EXPERTS * BLOCK, LANES), F32)

    sent = call(
        dispatch_kernel,
        (EXPERTS * BLOCK, LANES),
        *(ids, pltpu.with_memory_space_constraint(tokens, pltpu.HBM)),
        scratch=[pltpu.VMEM((2, n, LANES), BF16), pltpu.SemaphoreType.DMA((2,))],
        specs=(pltpu.VMEM, pltpu.HBM),
    )
    arrived = exchange(sent.reshape(EXPERTS, BLOCK, LANES), "expert").reshape(EXPERTS * BLOCK, LANES)
    rows = call(pack_kernel, (4, PART, LANES), arrived, scratch=[block_scratch, part_scratch])
    rows = exchange(rows, plane, quarter_groups(0))
    others = [lax.ppermute(rows, plane, across(mask, 0)) for mask in MASKS]
    total_shape, out_shape = ((2 * SIDE, 2 * WIDE), F32), ((4, PART, LANES), BF16)
    (total,) = call(functools.partial(first_kernel, 0), [total_shape], rows, weights, limit=32)
    for mask, other in zip(MASKS[:2], others[:2]):
        (total,) = call(functools.partial(next_kernel, mask), [total_shape], other, weights, held(total), limit=32)
    hidden, *outs = call(
        functools.partial(last_kernel, MASKS[2]),
        [((2 * SIDE, WIDE), BF16)] + [out_shape] * 3,
        *(others[2], weights, held(total), down),
        limit=32,
    )
    (partial,) = call(functools.partial(down_kernel, 0), [out_shape], held(hidden), down, limit=32)
    others = [lax.ppermute(out, plane, across(mask, 1)) for mask, out in zip(MASKS, outs)]
    for other, kind in zip(others, (F32, F32, BF16)):
        (partial,) = call(add_kernel, [((4, PART, LANES), kind)], held(partial), other, limit=24)
    partial = exchange(partial, plane, quarter_groups(1))
    summed = call(add_blocks_kernel, (EXPERTS * BLOCK, LANES), partial, scratch=[part_scratch, block_scratch])
    back = exchange(summed.reshape(EXPERTS, BLOCK, LANES), "expert").reshape(EXPERTS * BLOCK, LANES)
    (factors,) = call(gates_kernel, [((3, EXPERTS * BLOCK, 3 * n), BF16)], ids, gates)
    return call(combine_kernel, (width // DP, n), back, held(factors)).T


def solution(mesh):
    placed = (
        P(("expert", "tensor"), None),
        P("expert", None),
        P("expert", None),
        P("expert", ("dp", "tensor"), None),
        P("expert", ("dp", "tensor"), None),
        P("expert", ("dp", "tensor"), None),
    )
    return jax.shard_map(
        shards, mesh=mesh, in_specs=placed, out_specs=P(("expert", "tensor"), "dp"), check_vma=False
    )
```
